256 devices in a mesh: dom: 128 (over y, z, x), hid: 2 (over core).
Axes of the slice: x: 4, y: 4, z: 8, core: 2. Of those that a mesh axis runs over, the one named last changes fastest.
Arguments:
- feats: bfloat16 [524288, 256], P('dom', 'hid'), may hold values from -6 to 6
- adj_tiles: bfloat16 [32768, 128, 128], P('dom'), may hold values from -0.1875 to 0.1875
- adj_cols: int32 [4096, 8], P('dom'), may hold values from 0 to 63
- send_rows: int32 [16384, 32], P('dom'), may hold values from 0 to 4096, as said below
- weight: bfloat16 [256, 256], P('hid'), may hold values from -0.375 to 0.375
- bias: float32 [256], replicated, may hold values from -3 to 3
- cls_w: bfloat16 [256, 172], P('hid')
- labels: int32 [524288], P('dom'), may hold values from 0 to 171
Outputs:
- grad_feats: bfloat16 [524288, 256], P('dom', 'hid')
- grad_weight: float32 [256, 256], P('hid')
- grad_bias: float32 [256], replicated
- grad_cls: float32 [256, 172], P('hid')
The draws below stay inside these ranges and needn't reach their ends.
Inputs may be any that keep to these rules, and one draw needn't show every extreme that they name: `send_rows`: an entry 4096 marks an empty slot, others name a local row of the sender; live slots come first in each row. For every sender, the row for the peer one index above it (with wrap) is full.
All inputs are finite; a program needn't handle non-finite values.
Results may differ from the reference program's by a relative error of at most 0.019.
The reference program's roundings to bfloat16 on the way (of `extended`, `aggregate`, `hidden`, `logit_grad`, `preact_grad` and `agg_grad`) count: a program that leaves them out, or rounds other values in their place, can miss the bound.
Values may be sent and summed in bfloat16 or wider, within the bound.
No kernel may reach another device: no remote copies, remote signals or barrier semaphores. Data moves between devices by JAX's collectives and lax.ppermute only.
A program may use at most 128 MiB of HBM per device.

```python
import jax
import jax.numpy as jnp
from jax import lax

F = 256
C = 172
TILE = 128
NB_DEV = 32
K = 8
CAP = 32
ROWS_DEV = 4096
NODES = 524288
HALO = 4096
EXT_BLOCKS = 64
N_DOM = 128


def draw_send_rows(key, part):
    key = jax.random.fold_in(key, 3)
    key_rows, key_count = jax.random.split(key)
    pair_count = N_DOM * N_DOM
    local_rows = jax.random.randint(key_rows, (pair_count, CAP), 0, ROWS_DEV, dtype=jnp.int32)
    live_count = jax.random.randint(key_count, (pair_count, 1), 0, CAP + 1, dtype=jnp.int32)
    pair_index = jnp.arange(pair_count, dtype=jnp.int32)[:, None]
    sender = pair_index // N_DOM
    target = pair_index % N_DOM
    live_count = jnp.where(target == (sender + 1) % N_DOM, CAP, live_count)
    slot_index = jnp.arange(CAP, dtype=jnp.int32)[None, :]
    result = jnp.where(slot_index < live_count, local_rows, ROWS_DEV).astype(jnp.int32)
    result = result.at[0, 0].set(0)
    result = result.at[2, CAP - 1].set(ROWS_DEV)
    return result


def draw_cls_w(key, part):
    key = jax.random.fold_in(key, 7)
    key_base = jax.random.fold_in(key, 0)
    base = jax.random.normal(key_base, (F, C), jnp.float32) / jnp.sqrt(jnp.float32(F))
    return base.astype(jnp.bfloat16)


def plant(values, key, least, top_value):
    dims = values.shape
    spot = [jax.random.randint(jax.random.fold_in(key, axis), (), 0, dims[axis]) for axis in range(len(dims))]
    values = values.at[tuple(spot)].set(least)
    longest = dims.index(max(dims))
    spot[longest] = (spot[longest] + 1) % dims[longest]
    return values.at[tuple(spot)].set(top_value)


def levels(rng, extent, pieces, least, high):
    def one(dim, blocks):
        steps = jax.random.uniform(jax.random.fold_in(jax.random.fold_in(rng, 6), dim), (blocks,), jnp.float32, least / len(pieces), high / len(pieces))
        return jnp.repeat(jnp.exp(steps), extent[dim] // blocks).reshape((-1,) + (1,) * (len(extent) - dim - 1))

    gain = one(*pieces[0])
    for cut in pieces[1:]:
        gain = gain * one(*cut)
    return gain


def scatter_about(rng, extent, spread, bound, cuts=(), kind=jnp.bfloat16):
    values = jax.random.normal(rng, extent, jnp.float32) * spread
    if len(cuts) > 0:
        values = levels(rng, extent, cuts, -0.22, 0.18) * values
    return jnp.clip(values, min=-bound, max=bound).astype(kind)


def setup_inputs(seed: int = 0) -> dict:
    arg_keys = jax.random.split(jax.random.key(seed), 9)
    feats = scatter_about(arg_keys[0], (NODES, F), 1.0, 6.0, ((0, 128), (1, 2)))
    adj_tiles = scatter_about(arg_keys[1], (N_DOM * NB_DEV * K, TILE, TILE), (K * TILE) ** -0.5, 0.1875, ((0, 128),))
    adj_cols = plant(jax.random.randint(arg_keys[2], (N_DOM * NB_DEV, K), 0, EXT_BLOCKS), jax.random.fold_in(arg_keys[2], 1), 0, EXT_BLOCKS - 1).astype(jnp.int32)
    send_rows = draw_send_rows(jax.random.fold_in(arg_keys[8], 71), 0)
    weight = scatter_about(arg_keys[4], (F, F), F ** -0.5, 0.375, ((0, 2),))
    bias = scatter_about(arg_keys[5], (F,), 0.5, 3.0, (), jnp.float32)
    cls_w = draw_cls_w(jax.random.fold_in(arg_keys[8], 71), 0)
    labels = plant(jax.random.randint(arg_keys[7], (NODES,), 0, C), jax.random.fold_in(arg_keys[7], 1), 0, C - 1).astype(jnp.int32)
    return dict(feats=feats, adj_tiles=adj_tiles, adj_cols=adj_cols, send_rows=send_rows, weight=weight, bias=bias, cls_w=cls_w, labels=labels)


def reference(feats, adj_tiles, adj_cols, send_rows, weight, bias, cls_w, labels):
    row_count = NB_DEV * TILE
    slot_rows = send_rows.reshape(N_DOM, N_DOM, CAP)
    owners = jnp.arange(N_DOM, dtype=jnp.int32)[:, None, None]
    global_rows = jnp.where(slot_rows < row_count, owners * row_count + slot_rows, NODES).astype(jnp.int32)
    receiver_rows = jnp.transpose(global_rows, (1, 0, 2)).reshape(N_DOM, HALO)
    padded = jnp.concatenate([feats, jnp.zeros((1, F), feats.dtype)], 0)
    tile_blocks = adj_tiles.reshape(N_DOM, NB_DEV, K, TILE, TILE)
    col_ids = adj_cols.reshape(N_DOM, NB_DEV, K)
    local_feats = feats.reshape(N_DOM, row_count, F)

    def aggregate_one(operands):
        own_rows, blocks_here, ids_here, recv_here = operands
        extended = jnp.concatenate([own_rows, padded[recv_here]], 0).reshape(EXT_BLOCKS, TILE, F)
        selected = extended[ids_here].astype(jnp.float32)
        result = jnp.einsum("rkij,rkjf->rif", blocks_here.astype(jnp.float32), selected)
        return result.reshape(row_count, F).astype(jnp.bfloat16)

    aggregate = lax.map(aggregate_one, (local_feats, tile_blocks, col_ids, receiver_rows)).reshape(NODES, F)
    preact = jnp.dot(aggregate, weight, preferred_element_type=jnp.float32) + bias
    hidden = jax.nn.relu(preact).astype(jnp.bfloat16)
    logits = jnp.dot(hidden, cls_w, preferred_element_type=jnp.float32)
    onehot = (labels[:, None] == jnp.arange(C, dtype=jnp.int32)[None, :]).astype(jnp.float32)
    logit_grad = (jax.nn.softmax(logits, axis=-1) - onehot).astype(jnp.bfloat16)
    grad_cls = jnp.dot(hidden.T, logit_grad, preferred_element_type=jnp.float32) / NODES
    hidden_grad = jnp.dot(logit_grad, cls_w.T, preferred_element_type=jnp.float32)
    preact_grad = jnp.where(preact > 0, hidden_grad, 0.0).astype(jnp.bfloat16)
    grad_bias = jnp.sum(preact_grad.astype(jnp.float32), 0) / NODES
    grad_weight = jnp.dot(aggregate.T, preact_grad, preferred_element_type=jnp.float32) / NODES
    agg_grad = jnp.dot(preact_grad, weight.T, preferred_element_type=jnp.float32).astype(jnp.bfloat16)

    def transpose_one(operands):
        grad_rows, blocks_here, ids_here = operands
        row_blocks = grad_rows.reshape(NB_DEV, TILE, F).astype(jnp.float32)
        contrib = jnp.einsum("rkij,rif->rkjf", blocks_here.astype(jnp.float32), row_blocks)
        ext_grad = jax.ops.segment_sum(contrib.reshape(NB_DEV * K, TILE, F), ids_here.reshape(-1), num_segments=EXT_BLOCKS)
        ext_grad = ext_grad.reshape(EXT_BLOCKS * TILE, F)
        return ext_grad[:row_count], ext_grad[row_count:]

    local_grad, halo_grad = lax.map(transpose_one, (agg_grad.reshape(N_DOM, row_count, F), tile_blocks, col_ids))
    returned = jnp.zeros((NODES + 1, F), jnp.float32).at[receiver_rows.reshape(-1)].add(halo_grad.reshape(-1, F))
    grad_feats = (local_grad.reshape(NODES, F) + returned[:NODES]).astype(jnp.bfloat16)
    return (grad_feats, grad_weight, grad_bias, grad_cls)
```

```python
import jax
import jax.numpy as jnp
from jax import lax
from jax.experimental import pallas as pl
from jax.experimental.pallas import tpu as pltpu
from jax.sharding import PartitionSpec as P

F32 = jnp.float32
BF16 = jnp.bfloat16
MIB = 1 << 20
VMEM = pl.BlockSpec(memory_space=pltpu.VMEM)
SMEM = pl.BlockSpec(memory_space=pltpu.SMEM)
ANY = pl.BlockSpec(memory_space=pl.ANY)
NX, NY, NZ = 4, 4, 8
LINE = 128
SPAN = 512


def contract(a, b, da, db):
    return lax.dot_general(a, b, (((da,), (db,)), ((), ())), preferred_element_type=F32)


def gather_kernel(rows, feats, out, table, picked):
    peers, cap = rows.shape
    count = feats.shape[0]
    table[pl.ds(0, count), :] = feats[...].astype(F32)
    table[pl.ds(count, 8), :] = jnp.zeros((8, table.shape[1]), F32)

    def one_peer(p, carry):
        base = pl.multiple_of(p * cap, cap)
        for c in range(cap):
            picked[pl.ds(base + c, 1), :] = table[pl.ds(rows[p, c], 1), :]
        return carry

    lax.fori_loop(0, peers, one_peer, 0)
    out[...] = picked[...].astype(BF16)


def gather_rows(send_rows, feats):
    count, width = feats.shape
    slots = send_rows.size
    return pl.pallas_call(
        gather_kernel,
        out_shape=jax.ShapeDtypeStruct((slots, width), BF16),
        in_specs=[SMEM, VMEM],
        out_specs=VMEM,
        scratch_shapes=[pltpu.VMEM((count + 8, width), F32), pltpu.VMEM((slots, width), F32)],
        compiler_params=pltpu.CompilerParams(vmem_limit_bytes=24 * MIB),
        name="gather_rows",
    )(send_rows, feats)


def aggregate_kernel(cols, feats, halo, adj, agg, ext, tiles, sems):
    blocks, nonzero = cols.shape
    steps = sems.shape[0] - 2
    span = adj.shape[0] // steps
    own_copy = pltpu.make_async_copy(feats, ext.at[pl.ds(0, blocks)], sems.at[0])
    halo_copy = pltpu.make_async_copy(halo, ext.at[pl.ds(blocks, halo.shape[0])], sems.at[1])

    def tile_copy(i):
        return pltpu.make_async_copy(
            adj.at[pl.ds(i * span, span)], tiles.at[pl.ds(i * span, span)], sems.at[2 + i]
        )

    own_copy.start()
    halo_copy.start()
    for i in range(steps):
        tile_copy(i).start()
    own_copy.wait()
    halo_copy.wait()

    def one_step(i, carry):
        tile_copy(i).wait()
        for j in range(span // nonzero):
            r = i * (span // nonzero) + j
            left = jnp.concatenate([tiles[r * nonzero + k] for k in range(nonzero)], 1)
            right = jnp.concatenate([ext[cols[r, k]] for k in range(nonzero)], 0)
            agg[r] = contract(left, right, 1, 0).astype(BF16)
        return carry

    lax.fori_loop(0, steps, one_step, 0)


def aggregate_blocks(cols, feats, halo, adj):
    steps = 8
    return pl.pallas_call(
        aggregate_kernel,
        out_shape=jax.ShapeDtypeStruct(feats.shape, BF16),
        in_specs=[SMEM, ANY, ANY, ANY],
        out_specs=VMEM,
        scratch_shapes=[
            pltpu.VMEM((feats.shape[0] + halo.shape[0],) + feats.shape[1:], BF16),
            pltpu.VMEM(adj.shape, BF16),
            pltpu.SemaphoreType.DMA((2 + steps,)),
        ],
        compiler_params=pltpu.CompilerParams(vmem_limit_bytes=24 * MIB),
        name="aggregate_blocks",
    )(cols, feats, halo, adj)


def backward_kernel(
    classes, total_nodes, ids, cols, agg, other, weight_t, weight, cls, cls_t, bias, labels, adj,
    halo_out, own_out, share0, share1, share2, share3,
    ext_grad, tiles, packed, sum_w, sum_c, sum_b, sems, own_sem,
):
    blocks, nonzero = cols.shape
    tile = adj.shape[1]
    steps = sems.shape[0]
    span = adj.shape[0] // steps
    per_step = SPAN // tile
    hid = ids[0]

    def tile_copy(i):
        return pltpu.make_async_copy(
            adj.at[pl.ds(i * span, span)], tiles.at[pl.ds(i * span, span)], sems.at[i]
        )

    for i in range(steps):
        tile_copy(i).start()
    ext_grad[...] = jnp.zeros_like(ext_grad)
    sum_w[...] = jnp.zeros_like(sum_w)
    sum_c[...] = jnp.zeros_like(sum_c)
    sum_b[...] = jnp.zeros_like(sum_b)
    class_rows = cls_t.shape[0]
    class_id = lax.broadcasted_iota(jnp.int32, (class_rows, SPAN), 0)
    first = hid == 0
    half = agg.shape[1]

    def one_step(i, carry):
        nodes = pl.ds(pl.multiple_of(i * SPAN, SPAN), SPAN)
        mine = agg[nodes, :]
        theirs = other[nodes, :]
        both = jnp.concatenate(
            [jnp.where(first, mine, theirs), jnp.where(first, theirs, mine)], 1
        )
        preact = contract(weight_t[...], both, 1, 1) + jnp.tile(bias[...], (1, SPAN // bias.shape[1]))
        hidden = jnp.maximum(preact, 0.0).astype(BF16)
        logits = contract(cls_t[...], hidden, 1, 0)
        logits = jnp.where(class_id < classes, logits, -jnp.inf)
        powers = jnp.exp(logits - jnp.max(logits, 0, keepdims=True))
        share = powers / jnp.sum(powers, 0, keepdims=True)
        label = labels[pl.ds(i, 1), :]
        logit_grad = (share - jnp.where(class_id == label, 1.0, 0.0)).astype(BF16)
        hidden_grad = contract(cls[...], logit_grad, 1, 0)
        preact_grad = jnp.where(preact > 0, hidden_grad, 0.0).astype(BF16)
        own_hidden = jnp.where(first, hidden[:half], hidden[half:])
        sum_w[...] += contract(preact_grad, mine, 1, 0)
        sum_c[...] += contract(logit_grad, own_hidden, 1, 1)
        sum_b[...] += contract(jnp.ones((8, SPAN), BF16), preact_grad, 1, 1)
        agg_grad = contract(weight[...], preact_grad, 1, 0).astype(BF16)
        tile_copy(i).wait()
        for j in range(per_step):
            r = i * per_step + j
            right = jnp.concatenate([tiles[r * nonzero + k] for k in range(nonzero)], 1)
            term = contract(agg_grad[:, j * tile : (j + 1) * tile], right, 1, 0)
            for k in range(nonzero):
                ext_grad[cols[r, k]] += term[:, k * tile : (k + 1) * tile]
        return carry

    lax.fori_loop(0, steps, one_step, 0)
    own_copy = pltpu.make_async_copy(ext_grad.at[pl.ds(0, blocks)], own_out, own_sem)
    own_copy.start()

    def one_halo(b, carry):
        halo_out[b] = ext_grad[blocks + b].T.astype(BF16)
        return carry

    lax.fori_loop(0, halo_out.shape[0], one_halo, 0, unroll=4)
    scale = 1.0 / total_nodes
    units = 2 * half
    packed[pl.ds(0, units), :] = sum_w[...] * scale
    packed[pl.ds(units, class_rows), :] = sum_c[...] * scale
    packed[pl.ds(units + class_rows, 8), :] = sum_b[:, :half] * scale
    packed[pl.ds(units + class_rows + 8, 8), :] = sum_b[:, half:] * scale
    rest = units + class_rows + 16
    packed[pl.ds(rest, packed.shape[0] - rest), :] = jnp.zeros((packed.shape[0] - rest, half), F32)
    for d, target in enumerate((share0, share1, share2, share3)):
        start = pl.multiple_of(lax.rem(ids[1] + d, NX) * LINE, LINE)
        target[...] = packed[pl.ds(start, LINE), :]
    own_copy.wait()


def backward(ids, cols, agg, other, weight_t, weight, cls, cls_t, bias, labels, adj, classes, total_nodes):
    blocks = cols.shape[0]
    tile = adj.shape[1]
    rows, half = agg.shape
    steps = rows // SPAN
    class_rows = cls_t.shape[0]
    ext_blocks = 2 * blocks

    def body(*refs):
        backward_kernel(classes, total_nodes, *refs)

    share = jax.ShapeDtypeStruct((LINE, half), F32)
    return pl.pallas_call(
        body,
        out_shape=(
            jax.ShapeDtypeStruct((blocks, tile, half), BF16),
            jax.ShapeDtypeStruct((blocks, half, tile), F32),
        ) + (share,) * NX,
        in_specs=[SMEM, SMEM] + [VMEM] * 8 + [ANY],
        out_specs=(VMEM, ANY) + (VMEM,) * NX,
        scratch_shapes=[
            pltpu.VMEM((ext_blocks, half, tile), F32),
            pltpu.VMEM(adj.shape, BF16),
            pltpu.VMEM((NX * LINE, half), F32),
            pltpu.VMEM((2 * half, half), F32),
            pltpu.VMEM((class_rows, half), F32),
            pltpu.VMEM((8, 2 * half), F32),
            pltpu.SemaphoreType.DMA((steps,)),
            pltpu.SemaphoreType.DMA,
        ],
        compiler_params=pltpu.CompilerParams(vmem_limit_bytes=36 * MIB),
        name="backward",
    )(ids, cols, agg, other, weight_t, weight, cls, cls_t, bias, labels, adj)


def scatter_kernel(rows, arrived, own, out, values, *sums):
    peers, cap = rows.shape
    count, width = out.shape
    values[...] = arrived[...].astype(F32)
    for total in sums:
        total[...] = jnp.zeros_like(total)

    def one_peer(p, carry):
        base = pl.multiple_of(p * cap, cap)
        for c in range(cap):
            total = sums[c % len(sums)]
            row = pl.ds(rows[p, c], 1)
            total[row, :] = total[row, :] + values[pl.ds(base + c, 1), :]
        return carry

    lax.fori_loop(0, peers, one_peer, 0)
    result = own[...]
    for total in sums:
        result = result + total[pl.ds(0, count), :]
    out[...] = result.astype(BF16)


def scatter_rows(send_rows, arrived, own):
    count, width = own.shape
    lanes = 8
    return pl.pallas_call(
        scatter_kernel,
        out_shape=jax.ShapeDtypeStruct((count, width), BF16),
        in_specs=[SMEM, VMEM, VMEM],
        out_specs=VMEM,
        scratch_shapes=[pltpu.VMEM(arrived.shape, F32)]
        + [pltpu.VMEM((count + 8, width), F32)] * lanes,
        compiler_params=pltpu.CompilerParams(vmem_limit_bytes=36 * MIB),
        name="scatter_rows",
    )(send_rows, arrived, own)


def small_call(body, outs, ids, arrays, scratch, name):
    return pl.pallas_call(
        body,
        out_shape=outs,
        in_specs=[SMEM] + [VMEM] * len(arrays),
        out_specs=jax.tree.map(lambda _: VMEM, outs),
        scratch_shapes=[pltpu.VMEM(scratch, F32)],
        compiler_params=pltpu.CompilerParams(vmem_limit_bytes=4 * MIB),
        name=name,
    )(ids, *arrays)


def shift(value, axis, step):
    sizes = {"x": NX, "y": NY, "z": NZ}
    pairs = []
    for y in range(NY):
        for z in range(NZ):
            for x in range(NX):
                place = {"x": x, "y": y, "z": z}
                source = (y * NZ + z) * NX + x
                place[axis] = (place[axis] + step) % sizes[axis]
                pairs.append((source, (place["y"] * NZ + place["z"]) * NX + place["x"]))
    return lax.ppermute(value, "dom", pairs)


def sum_nodes(ids, shares, classes, half):
    got = [shares[0]] + [shift(shares[d], "x", d) for d in range(1, NX)]
    part = LINE // NY

    def split_y(ids, a, b, c, d, o0, o1, o2, o3, total):
        total[...] = (a[...] + b[...]) + (c[...] + d[...])
        for k, target in enumerate((o0, o1, o2, o3)):
            start = pl.multiple_of(lax.rem(ids[2] + k, NY) * part, part)
            target[...] = total[pl.ds(start, part), :]

    piece = jax.ShapeDtypeStruct((part, half), F32)
    pieces = small_call(split_y, (piece,) * NY, ids, got, (LINE, half), "split_y")
    got = [pieces[0]] + [shift(pieces[d], "y", d) for d in range(1, NY)]
    mine = (got[0] + got[1]) + (got[2] + got[3])
    got = [mine] + [shift(mine, "z", d) for d in range(1, NZ)]

    def sum_z(ids, *refs):
        out, slots = refs[NZ], refs[NZ + 1]
        for d in range(NZ):
            start = pl.multiple_of(lax.rem(ids[3] + NZ - d, NZ) * part, part)
            slots[pl.ds(start, part), :] = refs[d][...]
        total = slots[pl.ds(0, part), :]
        for k in range(1, NZ):
            total = total + slots[pl.ds(k * part, part), :]
        out[...] = total

    mine = small_call(sum_z, piece, ids, got, (NZ * part, half), "sum_z")
    got = [mine] + [shift(mine, "y", d) for d in range(1, NY)]

    def join_y(ids, a, b, c, d, out, unused):
        for k, source in enumerate((a, b, c, d)):
            start = pl.multiple_of(lax.rem(ids[2] + NY - k, NY) * part, part)
            out[pl.ds(start, part), :] = source[...]

    line = jax.ShapeDtypeStruct((LINE, half), F32)
    mine = small_call(join_y, line, ids, got, (8, half), "join_y")
    got = [mine] + [shift(mine, "x", d) for d in range(1, NX)]
    units = 2 * half
    class_rows = -(-classes // 8) * 8

    def join_x(ids, a, b, c, d, out_w, out_c, out_b, packed):
        for k, source in enumerate((a, b, c, d)):
            start = pl.multiple_of(lax.rem(ids[1] + NX - k, NX) * LINE, LINE)
            packed[pl.ds(start, LINE), :] = source[...]
        for k in range(units // half):
            out_w[:, k * half : (k + 1) * half] = packed[pl.ds(k * half, half), :].T
        out_c[:, :half] = packed[pl.ds(units, half), :].T
        out_c[:, half:] = packed[pl.ds(units + half, half), :].T[:, : classes - half]
        for k in range(units // half):
            row = units + class_rows + 8 * k
            out_b[:, k * half : (k + 1) * half] = packed[pl.ds(row, 8), :]

    outs = (
        jax.ShapeDtypeStruct((half, units), F32),
        jax.ShapeDtypeStruct((half, classes), F32),
        jax.ShapeDtypeStruct((8, units), F32),
    )
    grad_weight, grad_cls, grad_bias = small_call(
        join_x, outs, ids, got, (NX * LINE, half), "join_x"
    )
    return grad_weight, grad_cls, grad_bias[0]


def on_device(feats, adj_tiles, adj_cols, send_rows, weight, bias, cls_w, labels):
    row_count, half = feats.shape
    tile = adj_tiles.shape[1]
    blocks = adj_cols.shape[0]
    peers, cap = send_rows.shape
    classes = cls_w.shape[1]
    units = weight.shape[1]
    total_nodes = row_count * lax.axis_size("dom")
    swap = [(0, 1), (1, 0)]

    outgoing = gather_rows(send_rows, feats).reshape(peers, cap, half)
    incoming = lax.all_to_all(outgoing, "dom", split_axis=0, concat_axis=0, tiled=True)

    weight_l, cls_l, bias_l, labels_l, _ = lax.optimization_barrier(
        (weight, cls_w, bias, labels, outgoing)
    )
    hid = lax.axis_index("hid")
    dom = lax.axis_index("dom")
    ids = jnp.stack([hid, dom % NX, dom // (NX * NZ), (dom // NX) % NZ]).astype(jnp.int32)
    weight_o = lax.ppermute(weight_l, "hid", swap)
    cls_o = lax.ppermute(cls_l, "hid", swap)
    first = hid == 0
    weight_full = jnp.concatenate(
        [jnp.where(first, weight_l, weight_o), jnp.where(first, weight_o, weight_l)], 0
    )
    cls_full = jnp.concatenate(
        [jnp.where(first, cls_l, cls_o), jnp.where(first, cls_o, cls_l)], 0
    )
    class_rows = -(-classes // 8) * 8
    cls_full = jnp.pad(cls_full, ((0, 0), (0, class_rows - classes)))
    bias_wide = jnp.broadcast_to(bias_l[:, None], (units, 128))
    label_rows = labels_l.reshape(row_count // SPAN, SPAN)

    halo = incoming.reshape(blocks, tile, half)
    agg = aggregate_blocks(adj_cols, feats.reshape(blocks, tile, half), halo, adj_tiles)
    agg = agg.reshape(row_count, half)
    other = lax.ppermute(agg, "hid", swap)
    halo_grad, own_grad, *shares = backward(
        ids, adj_cols, agg, other, weight_full.T, weight_l, cls_full, cls_full.T, bias_wide,
        label_rows, adj_tiles, classes, total_nodes,
    )
    returned = halo_grad.reshape(peers, cap, half)
    arrived = lax.all_to_all(returned, "dom", split_axis=0, concat_axis=0, tiled=True)
    own = jnp.swapaxes(own_grad, 1, 2).reshape(row_count, half)
    grad_weight, grad_cls, grad_bias = sum_nodes(ids, shares, classes, half)
    grad_feats = scatter_rows(send_rows, arrived.reshape(row_count, half), own)
    return (grad_feats, grad_weight, grad_bias, grad_cls)


def solution(mesh):
    return jax.shard_map(
        on_device,
        mesh=mesh,
        in_specs=(
            P("dom", "hid"),
            P("dom", None, None),
            P("dom", None),
            P("dom", None),
            P("hid", None),
            P(),
            P("hid", None),
            P("dom"),
        ),
        out_specs=(P("dom", "hid"), P("hid", None), P(), P("hid", None)),
        check_vma=False,
    )
```

```python
import jax
import jax.numpy as jnp
from jax import lax
from jax.experimental import pallas as pl
from jax.experimental.pallas import tpu as pltpu
from jax.sharding import PartitionSpec as P

F32 = jnp.float32
BF16 = jnp.bfloat16
MIB = 1 << 20
VMEM = pl.BlockSpec(memory_space=pltpu.VMEM)
SMEM = pl.BlockSpec(memory_space=pltpu.SMEM)
ANY = pl.BlockSpec(memory_space=pl.ANY)
NX, NY, NZ = 4, 4, 8
PACKED = 512
SPAN = 512


def contract(a, b, da, db):
    return lax.dot_general(a, b, (((da,), (db,)), ((), ())), preferred_element_type=F32)


def gather_kernel(rows, feats, out, table, picked):
    peers, cap = rows.shape
    count = feats.shape[0]
    table[pl.ds(0, count), :] = feats[...].astype(F32)
    table[pl.ds(count, 8), :] = jnp.zeros((8, table.shape[1]), F32)

    def one_peer(p, carry):
        base = pl.multiple_of(p * cap, cap)
        for c in range(cap):
            picked[pl.ds(base + c, 1), :] = table[pl.ds(rows[p, c], 1), :]
        return carry

    lax.fori_loop(0, peers, one_peer, 0)
    out[...] = picked[...].astype(BF16)


def gather_rows(send_rows, feats):
    count, width = feats.shape
    slots = send_rows.size
    return pl.pallas_call(
        gather_kernel,
        out_shape=jax.ShapeDtypeStruct((slots, width), BF16),
        in_specs=[SMEM, VMEM],
        out_specs=VMEM,
        scratch_shapes=[pltpu.VMEM((count + 8, width), F32), pltpu.VMEM((slots, width), F32)],
        compiler_params=pltpu.CompilerParams(vmem_limit_bytes=24 * MIB),
        name="gather_rows",
    )(send_rows, feats)


def aggregate_kernel(cols, feats, halo, adj, agg, ext, tiles, sems):
    blocks, nonzero = cols.shape
    steps = sems.shape[0] - 2
    span = adj.shape[0] // steps
    own_copy = pltpu.make_async_copy(feats, ext.at[pl.ds(0, blocks)], sems.at[0])
    halo_copy = pltpu.make_async_copy(halo, ext.at[pl.ds(blocks, halo.shape[0])], sems.at[1])

    def tile_copy(i):
        return pltpu.make_async_copy(
            adj.at[pl.ds(i * span, span)], tiles.at[pl.ds(i * span, span)], sems.at[2 + i]
        )

    own_copy.start()
    halo_copy.start()
    for i in range(steps):
        tile_copy(i).start()
    own_copy.wait()
    halo_copy.wait()

    def one_step(i, carry):
        tile_copy(i).wait()
        for j in range(span // nonzero):
            r = i * (span // nonzero) + j
            left = jnp.concatenate([tiles[r * nonzero + k] for k in range(nonzero)], 1)
            right = jnp.concatenate([ext[cols[r, k]] for k in range(nonzero)], 0)
            agg[r] = contract(left, right, 1, 0).astype(BF16)
        return carry

    lax.fori_loop(0, steps, one_step, 0)


def aggregate_blocks(cols, feats, halo, adj):
    steps = 8
    return pl.pallas_call(
        aggregate_kernel,
        out_shape=jax.ShapeDtypeStruct(feats.shape, BF16),
        in_specs=[SMEM, ANY, ANY, ANY],
        out_specs=VMEM,
        scratch_shapes=[
            pltpu.VMEM((feats.shape[0] + halo.shape[0],) + feats.shape[1:], BF16),
            pltpu.VMEM(adj.shape, BF16),
            pltpu.SemaphoreType.DMA((2 + steps,)),
        ],
        compiler_params=pltpu.CompilerParams(vmem_limit_bytes=24 * MIB),
        name="aggregate_blocks",
    )(cols, feats, halo, adj)


def backward_kernel(
    classes, total_nodes, ids, cols, agg, other, weight_t, weight, cls, cls_t, bias, labels, adj,
    halo_out, own_out, packed,
    ext_grad, tiles, sum_w, sum_c, sum_b, sems, own_sem,
):
    blocks, nonzero = cols.shape
    tile = adj.shape[1]
    steps = sems.shape[0]
    span = adj.shape[0] // steps
    per_step = SPAN // tile
    hid = ids[0]

    def tile_copy(i):
        return pltpu.make_async_copy(
            adj.at[pl.ds(i * span, span)], tiles.at[pl.ds(i * span, span)], sems.at[i]
        )

    for i in range(steps):
        tile_copy(i).start()
    ext_grad[...] = jnp.zeros_like(ext_grad)
    sum_w[...] = jnp.zeros_like(sum_w)
    sum_c[...] = jnp.zeros_like(sum_c)
    sum_b[...] = jnp.zeros_like(sum_b)
    class_rows = cls_t.shape[0]
    class_id = lax.broadcasted_iota(jnp.int32, (class_rows, SPAN), 0)
    first = hid == 0
    half = agg.shape[1]

    def one_step(i, carry):
        nodes = pl.ds(pl.multiple_of(i * SPAN, SPAN), SPAN)
        mine = agg[nodes, :]
        theirs = other[nodes, :]
        both = jnp.concatenate(
            [jnp.where(first, mine, theirs), jnp.where(first, theirs, mine)], 1
        )
        preact = contract(weight_t[...], both, 1, 1) + jnp.tile(bias[...], (1, SPAN // bias.shape[1]))
        hidden = jnp.maximum(preact, 0.0).astype(BF16)
        logits = contract(cls_t[...], hidden, 1, 0)
        logits = jnp.where(class_id < classes, logits, -jnp.inf)
        powers = jnp.exp(logits - jnp.max(logits, 0, keepdims=True))
        share = powers / jnp.sum(powers, 0, keepdims=True)
        label = labels[pl.ds(i, 1), :]
        logit_grad = (share - jnp.where(class_id == label, 1.0, 0.0)).astype(BF16)
        hidden_grad = contract(cls[...], logit_grad, 1, 0)
        preact_grad = jnp.where(preact > 0, hidden_grad, 0.0).astype(BF16)
        own_hidden = jnp.where(first, hidden[:half], hidden[half:])
        sum_w[...] += contract(preact_grad, mine, 1, 0)
        sum_c[...] += contract(logit_grad, own_hidden, 1, 1)
        sum_b[...] += contract(jnp.ones((8, SPAN), BF16), preact_grad, 1, 1)
        agg_grad = contract(weight[...], preact_grad, 1, 0).astype(BF16)
        tile_copy(i).wait()
        for j in range(per_step):
            r = i * per_step + j
            right = jnp.concatenate([tiles[r * nonzero + k] for k in range(nonzero)], 1)
            term = contract(agg_grad[:, j * tile : (j + 1) * tile], right, 1, 0)
            for k in range(nonzero):
                ext_grad[cols[r, k]] += term[:, k * tile : (k + 1) * tile]
        return carry

    lax.fori_loop(0, steps, one_step, 0)
    own_copy = pltpu.make_async_copy(ext_grad.at[pl.ds(0, blocks)], own_out, own_sem)
    own_copy.start()

    def one_halo(b, carry):
        halo_out[b] = ext_grad[blocks + b].T.astype(BF16)
        return carry

    lax.fori_loop(0, halo_out.shape[0], one_halo, 0, unroll=4)
    scale = 1.0 / total_nodes
    units = 2 * half
    packed[pl.ds(0, units), :] = sum_w[...] * scale
    packed[pl.ds(units, class_rows), :] = sum_c[...] * scale
    packed[pl.ds(units + class_rows, 8), :] = sum_b[:, :half] * scale
    packed[pl.ds(units + class_rows + 8, 8), :] = sum_b[:, half:] * scale
    rest = units + class_rows + 16
    packed[pl.ds(rest, packed.shape[0] - rest), :] = jnp.zeros((packed.shape[0] - rest, half), F32)
    own_copy.wait()


def backward(ids, cols, agg, other, weight_t, weight, cls, cls_t, bias, labels, adj, classes, total_nodes):
    blocks = cols.shape[0]
    tile = adj.shape[1]
    rows, half = agg.shape
    steps = rows // SPAN
    class_rows = cls_t.shape[0]
    ext_blocks = 2 * blocks

    def body(*refs):
        backward_kernel(classes, total_nodes, *refs)

    return pl.pallas_call(
        body,
        out_shape=(
            jax.ShapeDtypeStruct((blocks, tile, half), BF16),
            jax.ShapeDtypeStruct((blocks, half, tile), F32),
            jax.ShapeDtypeStruct((PACKED, half), F32),
        ),
        in_specs=[SMEM, SMEM] + [VMEM] * 8 + [ANY],
        out_specs=(VMEM, ANY, VMEM),
        scratch_shapes=[
            pltpu.VMEM((ext_blocks, half, tile), F32),
            pltpu.VMEM(adj.shape, BF16),
            pltpu.VMEM((2 * half, half), F32),
            pltpu.VMEM((class_rows, half), F32),
            pltpu.VMEM((8, 2 * half), F32),
            pltpu.SemaphoreType.DMA((steps,)),
            pltpu.SemaphoreType.DMA,
        ],
        compiler_params=pltpu.CompilerParams(vmem_limit_bytes=36 * MIB),
        name="backward",
    )(ids, cols, agg, other, weight_t, weight, cls, cls_t, bias, labels, adj)


def scatter_kernel(rows, arrived, own, out, values, *sums):
    peers, cap = rows.shape
    count, width = out.shape
    values[...] = arrived[...].astype(F32)
    for total in sums:
        total[...] = jnp.zeros_like(total)

    def one_peer(p, carry):
        base = pl.multiple_of(p * cap, cap)
        for c in range(cap):
            total = sums[c % len(sums)]
            row = pl.ds(rows[p, c], 1)
            total[row, :] = total[row, :] + values[pl.ds(base + c, 1), :]
        return carry

    lax.fori_loop(0, peers, one_peer, 0)
    result = own[...]
    for total in sums:
        result = result + total[pl.ds(0, count), :]
    out[...] = result.astype(BF16)


def scatter_rows(send_rows, arrived, own):
    count, width = own.shape
    lanes = 8
    return pl.pallas_call(
        scatter_kernel,
        out_shape=jax.ShapeDtypeStruct((count, width), BF16),
        in_specs=[SMEM, VMEM, VMEM],
        out_specs=VMEM,
        scratch_shapes=[pltpu.VMEM(arrived.shape, F32)]
        + [pltpu.VMEM((count + 8, width), F32)] * lanes,
        compiler_params=pltpu.CompilerParams(vmem_limit_bytes=36 * MIB),
        name="scatter_rows",
    )(send_rows, arrived, own)


def move(value, axis, target):
    pairs = []
    for y in range(NY):
        for z in range(NZ):
            for x in range(NX):
                place = {"x": x, "y": y, "z": z}
                place[axis] = target(place[axis])
                pairs.append(
                    ((y * NZ + z) * NX + x, (place["y"] * NZ + place["z"]) * NX + place["x"])
                )
    return lax.ppermute(value, "dom", pairs)


def ahead(value, axis, step, size):
    return move(value, axis, lambda place: (place + step) % size)


def across(value, axis, flip):
    return move(value, axis, lambda place: place ^ flip)


def add_pairs(values):
    while len(values) > 1:
        values = [a + b for a, b in zip(values[::2], values[1::2])]
    return values[0]


def swap_shares(packed):
    groups = [
        [(y * NZ + z) * NX + x for z in range(NZ)] for y in range(NY) for x in range(NX)
    ]
    shares = packed.reshape(NZ, -1, packed.shape[1])
    return lax.all_to_all(
        shares, "dom", split_axis=0, concat_axis=0, tiled=True, axis_index_groups=groups
    )


def sum_xy(mine):
    for axis in ("x", "y"):
        mine = add_pairs([mine] + [across(mine, axis, flip) for flip in (1, 2, 3)])
    return mine


def finish(ids, mine, grad_feats, classes, units):
    part, half = mine.shape
    got = [mine] + [ahead(mine, "z", d, NZ) for d in range(1, NZ)]
    got, grad_feats = lax.optimization_barrier((got, grad_feats))
    class_rows = -(-classes // 16) * 16

    def body(ids, *refs):
        shares, (out_w, out_c, out_b, packed) = refs[:NZ], refs[NZ:]
        for d, share in enumerate(shares):
            start = pl.multiple_of(lax.rem(ids[1] + NZ - d, NZ) * part, part)
            packed[pl.ds(start, part), :] = share[...]
        for k in range(units // half):
            out_w[:, k * half : (k + 1) * half] = packed[pl.ds(k * half, half), :].T
        out_c[...] = packed[pl.ds(units, classes), :]
        for k in range(units // half):
            row = units + class_rows + 8 * k
            out_b[:, k * half : (k + 1) * half] = packed[pl.ds(row, 1), :]

    grad_weight, grad_cls, grad_bias = pl.pallas_call(
        body,
        out_shape=(
            jax.ShapeDtypeStruct((half, units), F32),
            jax.ShapeDtypeStruct((classes, half), F32),
            jax.ShapeDtypeStruct((1, units), F32),
        ),
        in_specs=[SMEM] + [VMEM] * NZ,
        out_specs=(VMEM,) * 3,
        scratch_shapes=[pltpu.VMEM((PACKED, half), F32)],
        compiler_params=pltpu.CompilerParams(vmem_limit_bytes=4 * MIB),
        name="finish",
    )(ids, *got)
    return grad_feats, grad_weight, grad_bias[0], grad_cls.T


def on_device(feats, adj_tiles, adj_cols, send_rows, weight, bias, cls_w, labels):
    row_count, half = feats.shape
    tile = adj_tiles.shape[1]
    blocks = adj_cols.shape[0]
    peers, cap = send_rows.shape
    classes = cls_w.shape[1]
    units = weight.shape[1]
    total_nodes = row_count * lax.axis_size("dom")
    swap = [(0, 1), (1, 0)]

    outgoing = gather_rows(send_rows, feats).reshape(peers, cap, half)
    incoming = lax.all_to_all(outgoing, "dom", split_axis=0, concat_axis=0, tiled=True)

    weight_l, cls_l, bias_l, labels_l, _ = lax.optimization_barrier(
        (weight, cls_w, bias, labels, outgoing)
    )
    hid = lax.axis_index("hid")
    dom = lax.axis_index("dom")
    ids = jnp.stack([hid, (dom // NX) % NZ]).astype(jnp.int32)
    weight_o = lax.ppermute(weight_l, "hid", swap)
    cls_o = lax.ppermute(cls_l, "hid", swap)
    first = hid == 0
    weight_full = jnp.concatenate(
        [jnp.where(first, weight_l, weight_o), jnp.where(first, weight_o, weight_l)], 0
    )
    cls_full = jnp.concatenate(
        [jnp.where(first, cls_l, cls_o), jnp.where(first, cls_o, cls_l)], 0
    )
    class_rows = -(-classes // 8) * 8
    cls_full = jnp.pad(cls_full, ((0, 0), (0, class_rows - classes)))
    bias_wide = jnp.broadcast_to(bias_l[:, None], (units, 128))
    label_rows = labels_l.reshape(row_count // SPAN, SPAN)

    halo = incoming.reshape(blocks, tile, half)
    agg = aggregate_blocks(adj_cols, feats.reshape(blocks, tile, half), halo, adj_tiles)
    agg = agg.reshape(row_count, half)
    other = lax.ppermute(agg, "hid", swap)
    halo_grad, own_grad, packed = backward(
        ids, adj_cols, agg, other, weight_full.T, weight_l, cls_full, cls_full.T, bias_wide,
        label_rows, adj_tiles, classes, total_nodes,
    )
    shares = swap_shares(packed)
    halo_grad, own_grad, shares = lax.optimization_barrier((halo_grad, own_grad, shares))
    returned = halo_grad.reshape(peers, cap, half)
    arrived = lax.all_to_all(returned, "dom", split_axis=0, concat_axis=0, tiled=True)
    own = jnp.swapaxes(own_grad, 1, 2).reshape(row_count, half)
    grad_feats = scatter_rows(send_rows, arrived.reshape(row_count, half), own)
    return finish(ids, sum_xy(shares.sum(0)), grad_feats, classes, units)


def solution(mesh):
    return jax.shard_map(
        on_device,
        mesh=mesh,
        in_specs=(
            P("dom", "hid"),
            P("dom", None, None),
            P("dom", None),
            P("dom", None),
            P("hid", None),
            P(),
            P("hid", None),
            P("dom"),
        ),
        out_specs=(P("dom", "hid"), P("hid", None), P(), P("hid", None)),
        check_vma=False,
    )
```

```python
import jax
import jax.numpy as jnp
from jax import lax
from jax.experimental import pallas as pl
from jax.experimental.pallas import tpu as pltpu
from jax.sharding import PartitionSpec as P

F32 = jnp.float32
BF16 = jnp.bfloat16
MIB = 1 << 20
VMEM = pl.BlockSpec(memory_space=pltpu.VMEM)
SMEM = pl.BlockSpec(memory_space=pltpu.SMEM)
HBM = pl.BlockSpec(memory_space=pltpu.HBM)
NX, NY, NZ = 4, 4, 8
PACKED = 512
TILE_STEPS = 8
SPAN = 512


def contract(a, b, da, db):
    return lax.dot_general(a, b, (((da,), (db,)), ((), ())), preferred_element_type=F32)


def in_hbm(value):
    return pltpu.with_memory_space_constraint(value, pltpu.HBM)


def gather_kernel(rows_hbm, feats_hbm, out, rows, feats, table, picked, row_sem, sems):
    cap, peers = rows.shape
    count = feats.shape[0]
    part = count // sems.shape[0]

    def part_copy(i):
        span = pl.ds(i * part, part)
        return pltpu.make_async_copy(feats_hbm.at[span], feats.at[span], sems.at[i])

    row_copy = pltpu.make_async_copy(rows_hbm, rows, row_sem)
    row_copy.start()
    for i in range(sems.shape[0]):
        part_copy(i).start()
    table[pl.ds(count, 8), :] = jnp.zeros((8, table.shape[1]), F32)
    for i in range(sems.shape[0]):
        span = pl.ds(i * part, part)
        part_copy(i).wait()
        table[span, :] = feats[span, :].astype(F32)
    row_copy.wait()

    def one_peer(p, carry):
        base = pl.multiple_of(p * cap, cap)
        for c in range(cap):
            picked[pl.ds(base + c, 1), :] = table[pl.ds(rows[c, p], 1), :]
        return carry

    lax.fori_loop(0, peers, one_peer, 0)
    out[...] = picked[...].astype(BF16)


def gather_rows(rows, feats):
    count, width = feats.shape
    slots = rows.size
    return pl.pallas_call(
        gather_kernel,
        out_shape=jax.ShapeDtypeStruct((slots, width), BF16),
        in_specs=[HBM, HBM],
        out_specs=VMEM,
        scratch_shapes=[
            pltpu.SMEM(rows.shape, rows.dtype),
            pltpu.VMEM(feats.shape, BF16),
            pltpu.VMEM((count + 8, width), F32),
            pltpu.VMEM((slots, width), F32),
            pltpu.SemaphoreType.DMA,
            pltpu.SemaphoreType.DMA((4,)),
        ],
        compiler_params=pltpu.CompilerParams(vmem_limit_bytes=12 * MIB),
        cost_estimate=pl.CostEstimate(flops=0, bytes_accessed=8 * MIB, transcendentals=0),
        name="gather_rows",
    )(in_hbm(rows), in_hbm(feats))


def tile_copy(adj, tiles, sems, i):
    span = pl.ds(i * (adj.shape[0] // sems.shape[0]), adj.shape[0] // sems.shape[0])
    return pltpu.make_async_copy(adj.at[span], tiles.at[span], sems.at[i])


def aggregate_kernel(cols, feats, halo, adj, agg, ext, tiles, sems):
    nonzero, blocks = cols.shape
    steps = sems.shape[0]
    per_step = blocks // steps
    for i in range(steps):
        tile_copy(adj, tiles, sems, i).start()
    ext[pl.ds(0, blocks)] = feats[...]
    ext[pl.ds(blocks, halo.shape[0])] = halo[...]

    def one_step(i, carry):
        tile_copy(adj, tiles, sems, i).wait()
        for j in range(per_step):
            r = i * per_step + j
            left = jnp.concatenate([tiles[r * nonzero + k] for k in range(nonzero)], 1)
            right = jnp.concatenate([ext[cols[k, r]] for k in range(nonzero)], 0)
            agg[r] = contract(left, right, 1, 0).astype(BF16)
        return carry

    lax.fori_loop(0, steps, one_step, 0)


def aggregate_blocks(cols, feats, halo, adj):
    return pl.pallas_call(
        aggregate_kernel,
        out_shape=jax.ShapeDtypeStruct(feats.shape, BF16),
        in_specs=[SMEM, VMEM, VMEM, HBM],
        out_specs=VMEM,
        scratch_shapes=[
            pltpu.VMEM((feats.shape[0] + halo.shape[0],) + feats.shape[1:], BF16),
            pltpu.VMEM(adj.shape, BF16),
            pltpu.SemaphoreType.DMA((TILE_STEPS,)),
        ],
        compiler_params=pltpu.CompilerParams(vmem_limit_bytes=24 * MIB),
        cost_estimate=pl.CostEstimate(flops=1 << 30, bytes_accessed=12 * MIB, transcendentals=0),
        name="aggregate_blocks",
    )(cols, feats, halo, in_hbm(adj))


def backward_kernel(
    classes, total_nodes, ids, cols, agg, other, weight_t, weight, cls, cls_t, bias, labels, adj,
    halo_out, own_out, packed,
    ext_grad, tiles, sum_w, sum_c, sum_b, sems, own_sem,
):
    nonzero, blocks = cols.shape
    tile = adj.shape[1]
    steps = sems.shape[0]
    span = adj.shape[0] // steps
    per_step = SPAN // tile
    hid = ids[0]

    def tile_copy(i):
        return pltpu.make_async_copy(
            adj.at[pl.ds(i * span, span)], tiles.at[pl.ds(i * span, span)], sems.at[i]
        )

    for i in range(steps):
        tile_copy(i).start()
    ext_grad[...] = jnp.zeros_like(ext_grad)
    sum_w[...] = jnp.zeros_like(sum_w)
    sum_c[...] = jnp.zeros_like(sum_c)
    sum_b[...] = jnp.zeros_like(sum_b)
    class_rows = cls_t.shape[0]
    class_id = lax.broadcasted_iota(jnp.int32, (class_rows, SPAN), 0)
    first = hid == 0
    half = agg.shape[1]

    def one_step(i, carry):
        nodes = pl.ds(pl.multiple_of(i * SPAN, SPAN), SPAN)
        mine = agg[nodes, :]
        theirs = other[nodes, :]
        both = jnp.concatenate(
            [jnp.where(first, mine, theirs), jnp.where(first, theirs, mine)], 1
        )
        preact = contract(weight_t[...], both, 1, 1) + jnp.tile(bias[...], (1, SPAN // bias.shape[1]))
        hidden = jnp.maximum(preact, 0.0).astype(BF16)
        logits = contract(cls_t[...], hidden, 1, 0)
        logits = jnp.where(class_id < classes, logits, -jnp.inf)
        powers = jnp.exp(logits - jnp.max(logits, 0, keepdims=True))
        share = powers / jnp.sum(powers, 0, keepdims=True)
        label = labels[pl.ds(i, 1), :]
        logit_grad = (share - jnp.where(class_id == label, 1.0, 0.0)).astype(BF16)
        hidden_grad = contract(cls[...], logit_grad, 1, 0)
        preact_grad = jnp.where(preact > 0, hidden_grad, 0.0).astype(BF16)
        own_hidden = jnp.where(first, hidden[:half], hidden[half:])
        sum_w[...] += contract(preact_grad, mine, 1, 0)
        sum_c[...] += contract(logit_grad, own_hidden, 1, 1)
        sum_b[...] += contract(jnp.ones((8, SPAN), BF16), preact_grad, 1, 1)
        agg_grad = contract(weight[...], preact_grad, 1, 0).astype(BF16)
        tile_copy(i).wait()
        for j in range(per_step):
            r = i * per_step + j
            right = jnp.concatenate([tiles[r * nonzero + k] for k in range(nonzero)], 1)
            term = contract(agg_grad[:, j * tile : (j + 1) * tile], right, 1, 0)
            for k in range(nonzero):
                ext_grad[cols[k, r]] += term[:, k * tile : (k + 1) * tile]
        return carry

    lax.fori_loop(0, steps, one_step, 0)
    own_copy = pltpu.make_async_copy(ext_grad.at[pl.ds(0, blocks)], own_out, own_sem)
    own_copy.start()

    def one_halo(b, carry):
        halo_out[b] = ext_grad[blocks + b].T.astype(BF16)
        return carry

    lax.fori_loop(0, halo_out.shape[0], one_halo, 0, unroll=4)
    scale = 1.0 / total_nodes
    units = 2 * half
    packed[pl.ds(0, units), :] = sum_w[...] * scale
    packed[pl.ds(units, class_rows), :] = sum_c[...] * scale
    packed[pl.ds(units + class_rows, 8), :] = sum_b[:, :half] * scale
    packed[pl.ds(units + class_rows + 8, 8), :] = sum_b[:, half:] * scale
    rest = units + class_rows + 16
    packed[pl.ds(rest, packed.shape[0] - rest), :] = jnp.zeros((packed.shape[0] - rest, half), F32)
    own_copy.wait()


def backward(ids, cols, agg, other, weight_t, weight, cls, cls_t, bias, labels, adj, classes, total_nodes):
    blocks = cols.shape[1]
    tile = adj.shape[1]
    rows, half = agg.shape
    steps = rows // SPAN
    class_rows = cls_t.shape[0]
    ext_blocks = 2 * blocks

    def body(*refs):
        backward_kernel(classes, total_nodes, *refs)

    return pl.pallas_call(
        body,
        out_shape=(
            jax.ShapeDtypeStruct((blocks, tile, half), BF16),
            pltpu.HBM((blocks, half, tile), F32),
            jax.ShapeDtypeStruct((PACKED, half), F32),
        ),
        in_specs=[SMEM, SMEM] + [VMEM] * 8 + [HBM],
        out_specs=(VMEM, HBM, VMEM),
        scratch_shapes=[
            pltpu.VMEM((ext_blocks, half, tile), F32),
            pltpu.VMEM(adj.shape, BF16),
            pltpu.VMEM((2 * half, half), F32),
            pltpu.VMEM((class_rows, half), F32),
            pltpu.VMEM((8, 2 * half), F32),
            pltpu.SemaphoreType.DMA((steps,)),
            pltpu.SemaphoreType.DMA,
        ],
        compiler_params=pltpu.CompilerParams(vmem_limit_bytes=36 * MIB),
        name="backward",
    )(ids, cols, agg, other, weight_t, weight, cls, cls_t, bias, labels, in_hbm(adj))


def scatter_kernel(rows_hbm, arrived, own, out, rows, values, row_sem, *sums):
    cap, peers = rows.shape
    count, width = out.shape
    row_copy = pltpu.make_async_copy(rows_hbm, rows, row_sem)
    row_copy.start()
    values[...] = arrived[...].astype(F32)
    sums[0][pl.ds(0, count), :] = own[...]
    for total in sums[1:]:
        total[...] = jnp.zeros_like(total)
    row_copy.wait()

    def one_peer(p, carry):
        base = pl.multiple_of(p * cap, cap)
        for c in range(cap):
            total = sums[c % len(sums)]
            row = pl.ds(rows[c, p], 1)
            total[row, :] = total[row, :] + values[pl.ds(base + c, 1), :]
        return carry

    lax.fori_loop(0, peers, one_peer, 0)
    result = sums[0][pl.ds(0, count), :]
    for total in sums[1:]:
        result = result + total[pl.ds(0, count), :]
    out[...] = result.astype(BF16)


def scatter_rows(rows, arrived, own):
    count, width = own.shape
    lanes = 8
    return pl.pallas_call(
        scatter_kernel,
        out_shape=jax.ShapeDtypeStruct((count, width), BF16),
        in_specs=[HBM, VMEM, VMEM],
        out_specs=VMEM,
        scratch_shapes=[
            pltpu.SMEM(rows.shape, rows.dtype),
            pltpu.VMEM(arrived.shape, F32),
            pltpu.SemaphoreType.DMA,
        ]
        + [pltpu.VMEM((count + 8, width), F32)] * lanes,
        compiler_params=pltpu.CompilerParams(vmem_limit_bytes=32 * MIB),
        cost_estimate=pl.CostEstimate(flops=0, bytes_accessed=8 * MIB, transcendentals=0),
        name="scatter_rows",
    )(in_hbm(rows), arrived, own)


def move(value, axis, target):
    pairs = []
    for y in range(NY):
        for z in range(NZ):
            for x in range(NX):
                place = {"x": x, "y": y, "z": z}
                place[axis] = target(place[axis])
                pairs.append(
                    ((y * NZ + z) * NX + x, (place["y"] * NZ + place["z"]) * NX + place["x"])
                )
    return lax.ppermute(value, "dom", pairs)


def ahead(value, axis, step, size):
    return move(value, axis, lambda place: (place + step) % size)


def across(value, axis, flip):
    return move(value, axis, lambda place: place ^ flip)


def add_pairs(values):
    while len(values) > 1:
        values = [a + b for a, b in zip(values[::2], values[1::2])]
    return values[0]


def swap_shares(packed):
    groups = [
        [(y * NZ + z) * NX + x for z in range(NZ)] for y in range(NY) for x in range(NX)
    ]
    shares = packed.reshape(NZ, -1, packed.shape[1])
    return lax.all_to_all(
        shares, "dom", split_axis=0, concat_axis=0, tiled=True, axis_index_groups=groups
    )


def sum_xy(mine):
    for axis in ("x", "y"):
        mine = add_pairs([mine] + [across(mine, axis, flip) for flip in (1, 2, 3)])
    return mine


def finish(ids, mine, grad_feats, classes, units):
    part, half = mine.shape
    got = [mine] + [ahead(mine, "z", d, NZ) for d in range(1, NZ)]
    got, grad_feats = lax.optimization_barrier((got, grad_feats))
    class_rows = -(-classes // 16) * 16

    def body(ids, *refs):
        shares, (out_w, out_c, out_b, packed) = refs[:NZ], refs[NZ:]
        for d, share in enumerate(shares):
            start = pl.multiple_of(lax.rem(ids[1] + NZ - d, NZ) * part, part)
            packed[pl.ds(start, part), :] = share[...]
        for k in range(units // half):
            out_w[:, k * half : (k + 1) * half] = packed[pl.ds(k * half, half), :].T
        out_c[...] = packed[pl.ds(units, classes), :]
        for k in range(units // half):
            row = units + class_rows + 8 * k
            out_b[:, k * half : (k + 1) * half] = packed[pl.ds(row, 1), :]

    grad_weight, grad_cls, grad_bias = pl.pallas_call(
        body,
        out_shape=(
            jax.ShapeDtypeStruct((half, units), F32),
            jax.ShapeDtypeStruct((classes, half), F32),
            jax.ShapeDtypeStruct((1, units), F32),
        ),
        in_specs=[SMEM] + [VMEM] * NZ,
        out_specs=(VMEM,) * 3,
        scratch_shapes=[pltpu.VMEM((PACKED, half), F32)],
        compiler_params=pltpu.CompilerParams(vmem_limit_bytes=4 * MIB),
        name="finish",
    )(ids, *got)
    return grad_feats, grad_weight, grad_bias[0], grad_cls.T


def on_device(feats, adj_tiles, adj_cols, send_rows, weight, bias, cls_w, labels):
    row_count, half = feats.shape
    tile = adj_tiles.shape[1]
    blocks = adj_cols.shape[0]
    peers, cap = send_rows.shape
    classes = cls_w.shape[1]
    units = weight.shape[1]
    total_nodes = row_count * lax.axis_size("dom")
    swap = [(0, 1), (1, 0)]

    rows = send_rows.T
    outgoing = gather_rows(rows, feats).reshape(peers, cap, half)
    incoming = lax.all_to_all(outgoing, "dom", split_axis=0, concat_axis=0, tiled=True)

    weight_l, cls_l, bias_l, labels_l, adj_cols, _ = lax.optimization_barrier(
        (weight, cls_w, bias, labels, adj_cols, outgoing)
    )
    cols = adj_cols.T
    hid = lax.axis_index("hid")
    dom = lax.axis_index("dom")
    ids = jnp.stack([hid, (dom // NX) % NZ]).astype(jnp.int32)
    weight_o = lax.ppermute(weight_l, "hid", swap)
    cls_o = lax.ppermute(cls_l, "hid", swap)
    first = hid == 0
    weight_full = jnp.concatenate(
        [jnp.where(first, weight_l, weight_o), jnp.where(first, weight_o, weight_l)], 0
    )
    cls_full = jnp.concatenate(
        [jnp.where(first, cls_l, cls_o), jnp.where(first, cls_o, cls_l)], 0
    )
    class_rows = -(-classes // 8) * 8
    cls_full = jnp.pad(cls_full, ((0, 0), (0, class_rows - classes)))
    bias_wide = jnp.broadcast_to(bias_l[:, None], (units, 128))
    label_rows = labels_l.reshape(row_count // SPAN, SPAN)

    weight_t = weight_full.T
    cls_t = cls_full.T
    incoming, cols, ids, weight_t, weight_l, cls_full, cls_t, bias_wide, label_rows = (
        lax.optimization_barrier(
            (incoming, cols, ids, weight_t, weight_l, cls_full, cls_t, bias_wide, label_rows)
        )
    )

    halo = incoming.reshape(blocks, tile, half)
    agg = aggregate_blocks(cols, feats.reshape(blocks, tile, half), halo, adj_tiles)
    agg = agg.reshape(row_count, half)
    other = lax.ppermute(agg, "hid", swap)
    halo_grad, own_grad, packed = backward(
        ids, cols, agg, other, weight_t, weight_l, cls_full, cls_t, bias_wide,
        label_rows, adj_tiles, classes, total_nodes,
    )
    shares = swap_shares(packed)
    halo_grad, own_grad, shares = lax.optimization_barrier((halo_grad, own_grad, shares))
    returned = halo_grad.reshape(peers, cap, half)
    arrived = lax.all_to_all(returned, "dom", split_axis=0, concat_axis=0, tiled=True)
    own = jnp.swapaxes(own_grad, 1, 2).reshape(row_count, half)
    grad_feats = scatter_rows(rows, arrived.reshape(row_count, half), own)
    return finish(ids, sum_xy(shares.sum(0)), grad_feats, classes, units)


def solution(mesh):
    return jax.shard_map(
        on_device,
        mesh=mesh,
        in_specs=(
            P("dom", "hid"),
            P("dom", None, None),
            P("dom", None),
            P("dom", None),
            P("hid", None),
            P(),
            P("hid", None),
            P("dom"),
        ),
        out_specs=(P("dom", "hid"), P("hid", None), P(), P("hid", None)),
        check_vma=False,
    )
```

```python
import jax
import jax.numpy as jnp
from jax import lax
from jax.experimental import pallas as pl
from jax.experimental.pallas import tpu as pltpu
from jax.sharding import PartitionSpec as P

F32 = jnp.float32
BF16 = jnp.bfloat16
MIB = 1 << 20
VMEM = pl.BlockSpec(memory_space=pltpu.VMEM)
SMEM = pl.BlockSpec(memory_space=pltpu.SMEM)
HBM = pl.BlockSpec(memory_space=pltpu.HBM)
NX, NY, NZ = 4, 4, 8
PACKED = 448
TILE_STEPS = 8
SPAN = 512


def contract(a, b, da, db):
    return lax.dot_general(a, b, (((da,), (db,)), ((), ())), preferred_element_type=F32)


def in_hbm(value):
    return pltpu.with_memory_space_constraint(value, pltpu.HBM)


def gather_kernel(rows_hbm, feats_hbm, out, rows, feats, table, picked, row_sem, sems):
    cap, peers = rows.shape
    count = feats.shape[0]
    part = count // sems.shape[0]

    def part_copy(i):
        span = pl.ds(i * part, part)
        return pltpu.make_async_copy(feats_hbm.at[span], feats.at[span], sems.at[i])

    row_copy = pltpu.make_async_copy(rows_hbm, rows, row_sem)
    row_copy.start()
    for i in range(sems.shape[0]):
        part_copy(i).start()
    table[pl.ds(count, 8), :] = jnp.zeros((8, table.shape[1]), F32)
    for i in range(sems.shape[0]):
        span = pl.ds(i * part, part)
        part_copy(i).wait()
        table[span, :] = feats[span, :].astype(F32)
    row_copy.wait()

    def one_peer(p, carry):
        base = pl.multiple_of(p * cap, cap)
        for c in range(cap):
            picked[pl.ds(base + c, 1), :] = table[pl.ds(rows[c, p], 1), :]
        return carry

    lax.fori_loop(0, peers, one_peer, 0)
    out[...] = picked[...].astype(BF16)


def gather_rows(rows, feats):
    count, width = feats.shape
    slots = rows.size
    return pl.pallas_call(
        gather_kernel,
        out_shape=jax.ShapeDtypeStruct((slots, width), BF16),
        in_specs=[HBM, HBM],
        out_specs=VMEM,
        scratch_shapes=[
            pltpu.SMEM(rows.shape, rows.dtype),
            pltpu.VMEM(feats.shape, BF16),
            pltpu.VMEM((count + 8, width), F32),
            pltpu.VMEM((slots, width), F32),
            pltpu.SemaphoreType.DMA,
            pltpu.SemaphoreType.DMA((4,)),
        ],
        compiler_params=pltpu.CompilerParams(vmem_limit_bytes=12 * MIB),
        cost_estimate=pl.CostEstimate(flops=0, bytes_accessed=8 * MIB, transcendentals=0),
        name="gather_rows",
    )(in_hbm(rows), in_hbm(feats))


def tile_copy(adj, tiles, sems, i):
    span = pl.ds(i * (adj.shape[0] // sems.shape[0]), adj.shape[0] // sems.shape[0])
    return pltpu.make_async_copy(adj.at[span], tiles.at[span], sems.at[i])


def aggregate_kernel(cols, feats, halo, adj, agg, ext, tiles, sems):
    nonzero, blocks = cols.shape
    steps = sems.shape[0]
    per_step = blocks // steps
    for i in range(steps):
        tile_copy(adj, tiles, sems, i).start()
    ext[pl.ds(0, blocks)] = feats[...]
    ext[pl.ds(blocks, halo.shape[0])] = halo[...]

    def one_step(i, carry):
        tile_copy(adj, tiles, sems, i).wait()
        for j in range(per_step):
            r = i * per_step + j
            left = jnp.concatenate([tiles[r * nonzero + k] for k in range(nonzero)], 1)
            right = jnp.concatenate([ext[cols[k, r]] for k in range(nonzero)], 0)
            agg[r] = contract(left, right, 1, 0).astype(BF16)
        return carry

    lax.fori_loop(0, steps, one_step, 0)


def aggregate_blocks(cols, feats, halo, adj):
    return pl.pallas_call(
        aggregate_kernel,
        out_shape=jax.ShapeDtypeStruct(feats.shape, BF16),
        in_specs=[SMEM, VMEM, VMEM, HBM],
        out_specs=VMEM,
        scratch_shapes=[
            pltpu.VMEM((feats.shape[0] + halo.shape[0],) + feats.shape[1:], BF16),
            pltpu.VMEM(adj.shape, BF16),
            pltpu.SemaphoreType.DMA((TILE_STEPS,)),
        ],
        compiler_params=pltpu.CompilerParams(vmem_limit_bytes=24 * MIB),
        cost_estimate=pl.CostEstimate(flops=1 << 30, bytes_accessed=12 * MIB, transcendentals=0),
        name="aggregate_blocks",
    )(cols, feats, halo, in_hbm(adj))


def dense_kernel(
    classes, total_nodes, ids, agg, other, weight_t, weight, cls, cls_t, bias, labels,
    grad_out, packed, sum_w, sum_c, sum_b,
):
    steps = labels.shape[0]
    class_rows = cls_t.shape[0]
    first = ids[0] == 0
    half = agg.shape[1]

    def both(mine, theirs, dim):
        return jnp.concatenate(
            [jnp.where(first, mine, theirs), jnp.where(first, theirs, mine)], dim
        )

    sum_w[...] = jnp.zeros_like(sum_w)
    sum_c[...] = jnp.zeros_like(sum_c)
    sum_b[...] = jnp.zeros_like(sum_b)
    class_id = lax.broadcasted_iota(jnp.int32, (class_rows, SPAN), 0)

    def one_step(i, carry):
        nodes = pl.ds(pl.multiple_of(i * SPAN, SPAN), SPAN)
        mine = agg[nodes, :]
        preact = contract(weight_t[...], both(mine, other[nodes, :], 1), 1, 1)
        preact = preact + jnp.tile(bias[...], (1, SPAN // bias.shape[1]))
        hidden = jnp.maximum(preact, 0.0).astype(BF16)
        logits = contract(cls_t[...], hidden, 1, 0)
        logits = jnp.where(class_id < classes, logits, -jnp.inf)
        powers = jnp.exp(logits - jnp.max(logits, 0, keepdims=True))
        share = powers / jnp.sum(powers, 0, keepdims=True)
        label = labels[pl.ds(i, 1), :]
        logit_grad = (share - jnp.where(class_id == label, 1.0, 0.0)).astype(BF16)
        hidden_grad = contract(cls[...], logit_grad, 1, 0)
        preact_grad = jnp.where(preact > 0, hidden_grad, 0.0).astype(BF16)
        own_hidden = jnp.where(first, hidden[:half], hidden[half:])
        sum_w[...] += contract(preact_grad, mine, 1, 0)
        sum_c[...] += contract(logit_grad, own_hidden, 1, 1)
        sum_b[...] += contract(jnp.ones((8, SPAN), BF16), preact_grad, 1, 1)
        agg_grad = contract(weight[...], preact_grad, 1, 0).astype(BF16)
        for j in range(SPAN // half):
            grad_out[i * (SPAN // half) + j] = agg_grad[:, j * half : (j + 1) * half]
        return carry

    lax.fori_loop(0, steps, one_step, 0)
    scale = 1.0 / total_nodes
    units = 2 * half
    packed[pl.ds(0, units), :] = sum_w[...] * scale
    packed[pl.ds(units, class_rows), :] = sum_c[...] * scale
    packed[pl.ds(units + class_rows, 8), :] = sum_b[:, :half] * scale
    packed[pl.ds(units + class_rows + 8, 8), :] = sum_b[:, half:] * scale


def dense(ids, agg, other, weight_t, weight, cls, cls_t, bias, labels, classes, total_nodes):
    rows, half = agg.shape
    units = weight.shape[1]
    steps = rows // SPAN
    class_rows = cls_t.shape[0]

    def body(*refs):
        dense_kernel(classes, total_nodes, *refs)

    return pl.pallas_call(
        body,
        out_shape=(
            jax.ShapeDtypeStruct((rows // half, half, half), BF16),
            jax.ShapeDtypeStruct((PACKED, half), F32),
        ),
        in_specs=[SMEM] + [VMEM] * 8,
        out_specs=(VMEM,) * 2,
        scratch_shapes=[
            pltpu.VMEM((units, half), F32),
            pltpu.VMEM((class_rows, half), F32),
            pltpu.VMEM((8, units), F32),
        ],
        compiler_params=pltpu.CompilerParams(vmem_limit_bytes=16 * MIB),
        cost_estimate=pl.CostEstimate(flops=5 << 30, bytes_accessed=4 * MIB, transcendentals=1 << 20),
        name="dense",
    )(ids, agg, other, weight_t, weight, cls, cls_t, bias, labels)


def spread_kernel(cols, grads, adj, halo_out, own_out, ext_grad, tiles, sems, own_sem):
    nonzero, blocks = cols.shape
    tile = adj.shape[1]
    steps = sems.shape[0]
    per_step = blocks // steps
    for i in range(steps):
        tile_copy(adj, tiles, sems, i).start()
    ext_grad[...] = jnp.zeros_like(ext_grad)

    def one_step(i, carry):
        tile_copy(adj, tiles, sems, i).wait()
        for j in range(per_step):
            r = i * per_step + j
            right = jnp.concatenate([tiles[r * nonzero + k] for k in range(nonzero)], 1)
            term = contract(grads[r], right, 1, 0)
            for k in range(nonzero):
                ext_grad[cols[k, r]] += term[:, k * tile : (k + 1) * tile]
        return carry

    lax.fori_loop(0, steps, one_step, 0)
    own_copy = pltpu.make_async_copy(ext_grad.at[pl.ds(0, blocks)], own_out, own_sem)
    own_copy.start()

    def one_halo(b, carry):
        halo_out[b] = ext_grad[blocks + b].T.astype(BF16)
        return carry

    lax.fori_loop(0, halo_out.shape[0], one_halo, 0, unroll=4)
    own_copy.wait()


def spread_blocks(cols, grads, adj):
    blocks = cols.shape[1]
    tile = adj.shape[1]
    half = grads.shape[1]
    return pl.pallas_call(
        spread_kernel,
        out_shape=(
            jax.ShapeDtypeStruct((blocks, tile, half), BF16),
            pltpu.HBM((blocks, half, tile), F32),
        ),
        in_specs=[SMEM, VMEM, HBM],
        out_specs=(VMEM, HBM),
        scratch_shapes=[
            pltpu.VMEM((2 * blocks, half, tile), F32),
            pltpu.VMEM(adj.shape, BF16),
            pltpu.SemaphoreType.DMA((TILE_STEPS,)),
            pltpu.SemaphoreType.DMA,
        ],
        compiler_params=pltpu.CompilerParams(vmem_limit_bytes=24 * MIB),
        cost_estimate=pl.CostEstimate(flops=1 << 30, bytes_accessed=12 * MIB, transcendentals=0),
        name="spread_blocks",
    )(cols, grads, in_hbm(adj))


def scatter_kernel(rows_hbm, arrived, own, out, rows, values, row_sem, *sums):
    cap, peers = rows.shape
    count, width = out.shape
    row_copy = pltpu.make_async_copy(rows_hbm, rows, row_sem)
    row_copy.start()
    values[...] = arrived[...].astype(F32)
    sums[0][pl.ds(0, count), :] = own[...]
    for total in sums[1:]:
        total[...] = jnp.zeros_like(total)
    row_copy.wait()

    def one_peer(p, carry):
        base = pl.multiple_of(p * cap, cap)
        for c in range(cap):
            total = sums[c % len(sums)]
            row = pl.ds(rows[c, p], 1)
            total[row, :] = total[row, :] + values[pl.ds(base + c, 1), :]
        return carry

    lax.fori_loop(0, peers, one_peer, 0)
    result = sums[0][pl.ds(0, count), :]
    for total in sums[1:]:
        result = result + total[pl.ds(0, count), :]
    out[...] = result.astype(BF16)


def scatter_rows(rows, arrived, own):
    count, width = own.shape
    lanes = 8
    return pl.pallas_call(
        scatter_kernel,
        out_shape=jax.ShapeDtypeStruct((count, width), BF16),
        in_specs=[HBM, VMEM, VMEM],
        out_specs=VMEM,
        scratch_shapes=[
            pltpu.SMEM(rows.shape, rows.dtype),
            pltpu.VMEM(arrived.shape, F32),
            pltpu.SemaphoreType.DMA,
        ]
        + [pltpu.VMEM((count + 8, width), F32)] * lanes,
        compiler_params=pltpu.CompilerParams(vmem_limit_bytes=32 * MIB),
        cost_estimate=pl.CostEstimate(flops=0, bytes_accessed=8 * MIB, transcendentals=0),
        name="scatter_rows",
    )(in_hbm(rows), arrived, own)


def move(value, axis, target):
    pairs = []
    for y in range(NY):
        for z in range(NZ):
            for x in range(NX):
                place = {"x": x, "y": y, "z": z}
                place[axis] = target(place[axis])
                pairs.append(
                    ((y * NZ + z) * NX + x, (place["y"] * NZ + place["z"]) * NX + place["x"])
                )
    return lax.ppermute(value, "dom", pairs)


def ahead(value, axis, step, size):
    return move(value, axis, lambda place: (place + step) % size)


def across(value, axis, flip):
    return move(value, axis, lambda place: place ^ flip)


def add_pairs(values):
    while len(values) > 1:
        values = [a + b for a, b in zip(values[::2], values[1::2])]
    return values[0]


def swap_shares(packed):
    groups = [
        [(y * NZ + z) * NX + x for z in range(NZ)] for y in range(NY) for x in range(NX)
    ]
    shares = packed.reshape(NZ, -1, packed.shape[1])
    return lax.all_to_all(
        shares, "dom", split_axis=0, concat_axis=0, tiled=True, axis_index_groups=groups
    )


def sum_xy(mine):
    for axis in ("x", "y"):
        mine = add_pairs([mine] + [across(mine, axis, flip) for flip in (1, 2, 3)])
    return mine


def finish(ids, mine, grad_feats, classes, units):
    part, half = mine.shape
    got = [mine] + [ahead(mine, "z", d, NZ) for d in range(1, NZ)]
    got, grad_feats = lax.optimization_barrier((got, grad_feats))
    class_rows = -(-classes // 16) * 16

    def body(ids, *refs):
        shares, (out_w, out_c, out_b, packed) = refs[:NZ], refs[NZ:]
        for d, share in enumerate(shares):
            start = pl.multiple_of(lax.rem(ids[1] + NZ - d, NZ) * part, part)
            packed[pl.ds(start, part), :] = share[...]
        for k in range(units // half):
            out_w[:, k * half : (k + 1) * half] = packed[pl.ds(k * half, half), :].T
        out_c[...] = packed[pl.ds(units, classes), :]
        for k in range(units // half):
            row = units + class_rows + 8 * k
            out_b[:, k * half : (k + 1) * half] = packed[pl.ds(row, 1), :]

    grad_weight, grad_cls, grad_bias = pl.pallas_call(
        body,
        out_shape=(
            jax.ShapeDtypeStruct((half, units), F32),
            jax.ShapeDtypeStruct((classes, half), F32),
            jax.ShapeDtypeStruct((1, units), F32),
        ),
        in_specs=[SMEM] + [VMEM] * NZ,
        out_specs=(VMEM,) * 3,
        scratch_shapes=[pltpu.VMEM((PACKED, half), F32)],
        compiler_params=pltpu.CompilerParams(vmem_limit_bytes=4 * MIB),
        name="finish",
    )(ids, *got)
    return grad_feats, grad_weight, grad_bias[0], grad_cls.T


def on_device(feats, adj_tiles, adj_cols, send_rows, weight, bias, cls_w, labels):
    row_count, half = feats.shape
    tile = adj_tiles.shape[1]
    blocks = adj_cols.shape[0]
    peers, cap = send_rows.shape
    classes = cls_w.shape[1]
    units = weight.shape[1]
    total_nodes = row_count * lax.axis_size("dom")
    swap = [(0, 1), (1, 0)]

    rows = send_rows.T
    outgoing = gather_rows(rows, feats).reshape(peers, cap, half)
    incoming = lax.all_to_all(outgoing, "dom", split_axis=0, concat_axis=0, tiled=True)

    weight_l, cls_l, bias_l, labels_l, adj_cols, _ = lax.optimization_barrier(
        (weight, cls_w, bias, labels, adj_cols, outgoing)
    )
    cols = adj_cols.T
    hid = lax.axis_index("hid")
    dom = lax.axis_index("dom")
    ids = jnp.stack([hid, (dom // NX) % NZ]).astype(jnp.int32)
    weight_o = lax.ppermute(weight_l, "hid", swap)
    cls_o = lax.ppermute(cls_l, "hid", swap)
    first = hid == 0
    weight_full = jnp.concatenate(
        [jnp.where(first, weight_l, weight_o), jnp.where(first, weight_o, weight_l)], 0
    )
    cls_full = jnp.concatenate(
        [jnp.where(first, cls_l, cls_o), jnp.where(first, cls_o, cls_l)], 0
    )
    class_rows = -(-classes // 8) * 8
    cls_full = jnp.pad(cls_full, ((0, 0), (0, class_rows - classes)))
    bias_wide = jnp.broadcast_to(bias_l[:, None], (units, 128))
    label_rows = labels_l.reshape(row_count // SPAN, SPAN)

    weight_t = weight_full.T
    cls_t = cls_full.T
    incoming, cols, ids, weight_t, weight_l, cls_full, cls_t, bias_wide, label_rows = (
        lax.optimization_barrier(
            (incoming, cols, ids, weight_t, weight_l, cls_full, cls_t, bias_wide, label_rows)
        )
    )

    halo = incoming.reshape(blocks, tile, half)
    agg = aggregate_blocks(cols, feats.reshape(blocks, tile, half), halo, adj_tiles)
    agg = agg.reshape(row_count, half)
    other = lax.ppermute(agg, "hid", swap)
    grads, packed = dense(
        ids, agg, other, weight_t, weight_l, cls_full, cls_t, bias_wide, label_rows,
        classes, total_nodes,
    )
    halo_grad, own_grad = spread_blocks(cols, grads, adj_tiles)
    shares = swap_shares(packed)
    halo_grad, own_grad, shares = lax.optimization_barrier((halo_grad, own_grad, shares))
    returned = halo_grad.reshape(peers, cap, half)
    arrived = lax.all_to_all(returned, "dom", split_axis=0, concat_axis=0, tiled=True)
    own = jnp.swapaxes(own_grad, 1, 2).reshape(row_count, half)
    grad_feats = scatter_rows(rows, arrived.reshape(row_count, half), own)
    return finish(ids, sum_xy(shares.sum(0)), grad_feats, classes, units)


def solution(mesh):
    return jax.shard_map(
        on_device,
        mesh=mesh,
        in_specs=(
            P("dom", "hid"),
            P("dom", None, None),
            P("dom", None),
            P("dom", None),
            P("hid", None),
            P(),
            P("hid", None),
            P("dom"),
        ),
        out_specs=(P("dom", "hid"), P("hid", None), P(), P("hid", None)),
        check_vma=False,
    )
```

```python
import jax
import jax.numpy as jnp
from jax import lax
from jax.experimental import pallas as pl
from jax.experimental.pallas import tpu as pltpu
from jax.sharding import PartitionSpec as P

F32 = jnp.float32
BF16 = jnp.bfloat16
MIB = 1 << 20
VMEM = pl.BlockSpec(memory_space=pltpu.VMEM)
SMEM = pl.BlockSpec(memory_space=pltpu.SMEM)
HBM = pl.BlockSpec(memory_space=pltpu.HBM)
NX, NY, NZ = 4, 4, 8
PACKED = 448
TILE_STEPS = 8
SPAN = 2048


def contract(a, b, da, db):
    return lax.dot_general(a, b, (((da,), (db,)), ((), ())), preferred_element_type=F32)


def in_hbm(value):
    return pltpu.with_memory_space_constraint(value, pltpu.HBM)


def gather_kernel(rows_hbm, feats_hbm, out, rows, feats, table, picked, ready, row_sem, sems, out_sems):
    cap, peers = rows.shape
    count = feats.shape[0]
    part = count // sems.shape[0]
    some = peers // out_sems.shape[0]

    def part_copy(i):
        span = pl.ds(i * part, part)
        return pltpu.make_async_copy(feats_hbm.at[span], feats.at[span], sems.at[i])

    def out_copy(i):
        span = pl.ds(i * some * cap, some * cap)
        return pltpu.make_async_copy(ready.at[span], out.at[span], out_sems.at[i])

    row_copy = pltpu.make_async_copy(rows_hbm, rows, row_sem)
    row_copy.start()
    for i in range(sems.shape[0]):
        part_copy(i).start()
    table[pl.ds(count, 8), :] = jnp.zeros((8, table.shape[1]), F32)
    for i in range(sems.shape[0]):
        span = pl.ds(i * part, part)
        part_copy(i).wait()
        table[span, :] = feats[span, :].astype(F32)
    row_copy.wait()

    def one_peer(p, carry):
        base = pl.multiple_of(p * cap, cap)
        for c in range(cap):
            picked[pl.ds(base + c, 1), :] = table[pl.ds(rows[c, p], 1), :]
        return carry

    for i in range(out_sems.shape[0]):
        lax.fori_loop(i * some, (i + 1) * some, one_peer, 0)
        span = pl.ds(i * some * cap, some * cap)
        ready[span, :] = picked[span, :].astype(BF16)
        out_copy(i).start()
    for i in range(out_sems.shape[0]):
        out_copy(i).wait()


def gather_rows(rows, feats):
    count, width = feats.shape
    slots = rows.size
    return pl.pallas_call(
        gather_kernel,
        out_shape=pltpu.HBM((slots, width), BF16),
        in_specs=[HBM, HBM],
        out_specs=HBM,
        scratch_shapes=[
            pltpu.SMEM(rows.shape, rows.dtype),
            pltpu.VMEM(feats.shape, BF16),
            pltpu.VMEM((count + 8, width), F32),
            pltpu.VMEM((slots, width), F32),
            pltpu.VMEM((slots, width), BF16),
            pltpu.SemaphoreType.DMA,
            pltpu.SemaphoreType.DMA((4,)),
            pltpu.SemaphoreType.DMA((4,)),
        ],
        compiler_params=pltpu.CompilerParams(vmem_limit_bytes=12 * MIB),
        cost_estimate=pl.CostEstimate(flops=0, bytes_accessed=8 * MIB, transcendentals=0),
        name="gather_rows",
    )(in_hbm(rows), in_hbm(feats))


def tile_copy(adj, tiles, sems, i):
    span = pl.ds(i * (adj.shape[0] // sems.shape[0]), adj.shape[0] // sems.shape[0])
    return pltpu.make_async_copy(adj.at[span], tiles.at[span], sems.at[i])


def aggregate_kernel(cols, feats, halo, adj, agg, ext, tiles, sems):
    nonzero, blocks = cols.shape
    steps = sems.shape[0]
    per_step = blocks // steps
    for i in range(steps):
        tile_copy(adj, tiles, sems, i).start()
    ext[pl.ds(0, blocks)] = feats[...]
    ext[pl.ds(blocks, halo.shape[0])] = halo[...]

    def one_step(i, carry):
        tile_copy(adj, tiles, sems, i).wait()
        for j in range(per_step):
            r = i * per_step + j
            left = jnp.concatenate([tiles[r * nonzero + k] for k in range(nonzero)], 1)
            right = jnp.concatenate([ext[cols[k, r]] for k in range(nonzero)], 0)
            agg[r] = contract(left, right, 1, 0).astype(BF16)
        return carry

    lax.fori_loop(0, steps, one_step, 0)


def aggregate_blocks(cols, feats, halo, adj):
    return pl.pallas_call(
        aggregate_kernel,
        out_shape=jax.ShapeDtypeStruct(feats.shape, BF16),
        in_specs=[SMEM, VMEM, VMEM, HBM],
        out_specs=VMEM,
        scratch_shapes=[
            pltpu.VMEM((feats.shape[0] + halo.shape[0],) + feats.shape[1:], BF16),
            pltpu.VMEM(adj.shape, BF16),
            pltpu.SemaphoreType.DMA((TILE_STEPS,)),
        ],
        compiler_params=pltpu.CompilerParams(vmem_limit_bytes=24 * MIB),
        cost_estimate=pl.CostEstimate(flops=1 << 30, bytes_accessed=12 * MIB, transcendentals=0),
        name="aggregate_blocks",
    )(cols, feats, halo, in_hbm(adj))


def dense_kernel(
    classes, total_nodes, ids, agg, other, weight, weight_o, class_t, class_o, bias_row, labels,
    grad_out, packed,
    sum_w, sum_c, sum_b, weight_t, cls_t, cls, bias,
):
    steps = labels.shape[0]
    class_rows = cls_t.shape[0]
    first = ids[0] == 0
    half = agg.shape[1]

    def both(mine, theirs, dim):
        return jnp.concatenate(
            [jnp.where(first, mine, theirs), jnp.where(first, theirs, mine)], dim
        )

    weight_t[...] = both(weight[...], weight_o[...], 0).T
    cls_t[...] = both(class_t[...], class_o[...], 1)
    cls[...] = cls_t[...].T
    bias[...] = jnp.broadcast_to(bias_row[...], (128, 2 * half)).T
    sum_w[...] = jnp.zeros_like(sum_w)
    sum_c[...] = jnp.zeros_like(sum_c)
    sum_b[...] = jnp.zeros_like(sum_b)
    class_id = lax.broadcasted_iota(jnp.int32, (class_rows, SPAN), 0)

    def one_step(i, carry):
        nodes = pl.ds(pl.multiple_of(i * SPAN, SPAN), SPAN)
        mine = agg[nodes, :]
        preact = contract(weight_t[...], both(mine, other[nodes, :], 1), 1, 1)
        preact = preact + jnp.tile(bias[...], (1, SPAN // bias.shape[1]))
        hidden = jnp.maximum(preact, 0.0).astype(BF16)
        logits = contract(cls_t[...], hidden, 1, 0)
        logits = jnp.where(class_id < classes, logits, -jnp.inf)
        powers = jnp.exp(logits - jnp.max(logits, 0, keepdims=True))
        share = powers * (1.0 / jnp.sum(powers, 0, keepdims=True))
        label = labels[pl.ds(i, 1), :]
        logit_grad = (share - jnp.where(class_id == label, 1.0, 0.0)).astype(BF16)
        hidden_grad = contract(cls[...], logit_grad, 1, 0)
        preact_grad = jnp.where(preact > 0, hidden_grad, 0.0).astype(BF16)
        own_hidden = jnp.where(first, hidden[:half], hidden[half:])
        sum_w[...] += contract(preact_grad, mine, 1, 0)
        sum_c[...] += contract(logit_grad, own_hidden, 1, 1)
        sum_b[...] += contract(jnp.ones((8, SPAN), BF16), preact_grad, 1, 1)
        agg_grad = contract(weight[...], preact_grad, 1, 0).astype(BF16)
        for j in range(SPAN // half):
            grad_out[i * (SPAN // half) + j] = agg_grad[:, j * half : (j + 1) * half]
        return carry

    lax.fori_loop(0, steps, one_step, 0)
    scale = 1.0 / total_nodes
    units = 2 * half
    packed[pl.ds(0, units), :] = sum_w[...] * scale
    packed[pl.ds(units, class_rows), :] = sum_c[...] * scale
    packed[pl.ds(units + class_rows, 8), :] = sum_b[:, :half] * scale
    packed[pl.ds(units + class_rows + 8, 8), :] = sum_b[:, half:] * scale


def dense(ids, agg, other, weight, weight_o, class_t, class_o, bias_row, labels, classes, total_nodes):
    rows, half = agg.shape
    units = weight.shape[1]
    steps = rows // SPAN
    class_rows = class_t.shape[0]

    def body(*refs):
        dense_kernel(classes, total_nodes, *refs)

    return pl.pallas_call(
        body,
        out_shape=(
            jax.ShapeDtypeStruct((rows // half, half, half), BF16),
            jax.ShapeDtypeStruct((PACKED, half), F32),
        ),
        in_specs=[SMEM] + [VMEM] * 8,
        out_specs=(VMEM,) * 2,
        scratch_shapes=[
            pltpu.VMEM((units, half), F32),
            pltpu.VMEM((class_rows, half), F32),
            pltpu.VMEM((8, units), F32),
            pltpu.VMEM((units, 2 * half), BF16),
            pltpu.VMEM((class_rows, units), BF16),
            pltpu.VMEM((units, class_rows), BF16),
            pltpu.VMEM((units, 128), F32),
        ],
        compiler_params=pltpu.CompilerParams(vmem_limit_bytes=32 * MIB),
        cost_estimate=pl.CostEstimate(flops=5 << 30, bytes_accessed=4 * MIB, transcendentals=1 << 20),
        name="dense",
    )(ids, agg, other, weight, weight_o, class_t, class_o, bias_row, labels)


def spread_kernel(cols, grads, adj, halo_out, own_out, ext_grad, tiles, sems, own_sem):
    nonzero, blocks = cols.shape
    tile = adj.shape[1]
    steps = sems.shape[0]
    per_step = blocks // steps
    for i in range(steps):
        tile_copy(adj, tiles, sems, i).start()
    ext_grad[...] = jnp.zeros_like(ext_grad)

    def one_step(i, carry):
        tile_copy(adj, tiles, sems, i).wait()
        for j in range(per_step):
            r = i * per_step + j
            right = jnp.concatenate([tiles[r * nonzero + k] for k in range(nonzero)], 1)
            term = contract(grads[r], right, 1, 0)
            for k in range(nonzero):
                ext_grad[cols[k, r]] += term[:, k * tile : (k + 1) * tile]
        return carry

    lax.fori_loop(0, steps, one_step, 0)
    own_copy = pltpu.make_async_copy(ext_grad.at[pl.ds(0, blocks)], own_out, own_sem)
    own_copy.start()

    def one_halo(b, carry):
        halo_out[b] = ext_grad[blocks + b].T.astype(BF16)
        return carry

    lax.fori_loop(0, halo_out.shape[0], one_halo, 0, unroll=4)
    own_copy.wait()


def spread_blocks(cols, grads, adj):
    blocks = cols.shape[1]
    tile = adj.shape[1]
    half = grads.shape[1]
    return pl.pallas_call(
        spread_kernel,
        out_shape=(
            jax.ShapeDtypeStruct((blocks, tile, half), BF16),
            pltpu.HBM((blocks, half, tile), F32),
        ),
        in_specs=[SMEM, VMEM, HBM],
        out_specs=(VMEM, HBM),
        scratch_shapes=[
            pltpu.VMEM((2 * blocks, half, tile), F32),
            pltpu.VMEM(adj.shape, BF16),
            pltpu.SemaphoreType.DMA((TILE_STEPS,)),
            pltpu.SemaphoreType.DMA,
        ],
        compiler_params=pltpu.CompilerParams(vmem_limit_bytes=24 * MIB),
        cost_estimate=pl.CostEstimate(flops=1 << 30, bytes_accessed=12 * MIB, transcendentals=0),
        name="spread_blocks",
    )(cols, grads, in_hbm(adj))


def scatter_kernel(rows_hbm, arrived, own, out, rows, values, ready, row_sem, out_sems, *sums):
    cap, peers = rows.shape
    count, width = out.shape
    row_copy = pltpu.make_async_copy(rows_hbm, rows, row_sem)
    row_copy.start()
    values[...] = arrived[...].astype(F32)
    sums[0][pl.ds(0, count), :] = own[...]
    for total in sums[1:]:
        total[...] = jnp.zeros_like(total)
    row_copy.wait()

    def one_peer(p, carry):
        base = pl.multiple_of(p * cap, cap)
        for c in range(cap):
            total = sums[c % len(sums)]
            row = pl.ds(rows[c, p], 1)
            total[row, :] = total[row, :] + values[pl.ds(base + c, 1), :]
        return carry

    lax.fori_loop(0, peers, one_peer, 0)
    part = count // out_sems.shape[0]

    def out_copy(i):
        span = pl.ds(i * part, part)
        return pltpu.make_async_copy(ready.at[span], out.at[span], out_sems.at[i])

    for i in range(out_sems.shape[0]):
        span = pl.ds(i * part, part)
        result = sums[0][span, :]
        for total in sums[1:]:
            result = result + total[span, :]
        ready[span, :] = result.astype(BF16)
        out_copy(i).start()
    for i in range(out_sems.shape[0]):
        out_copy(i).wait()


def scatter_rows(rows, arrived, own):
    count, width = own.shape
    lanes = 8
    return pl.pallas_call(
        scatter_kernel,
        out_shape=pltpu.HBM((count, width), BF16),
        in_specs=[HBM, VMEM, VMEM],
        out_specs=HBM,
        scratch_shapes=[
            pltpu.SMEM(rows.shape, rows.dtype),
            pltpu.VMEM(arrived.shape, F32),
            pltpu.VMEM((count, width), BF16),
            pltpu.SemaphoreType.DMA,
            pltpu.SemaphoreType.DMA((4,)),
        ]
        + [pltpu.VMEM((count + 8, width), F32)] * lanes,
        compiler_params=pltpu.CompilerParams(vmem_limit_bytes=32 * MIB),
        cost_estimate=pl.CostEstimate(flops=0, bytes_accessed=8 * MIB, transcendentals=0),
        name="scatter_rows",
    )(in_hbm(rows), arrived, own)


def move(value, axis, target):
    pairs = []
    for y in range(NY):
        for z in range(NZ):
            for x in range(NX):
                place = {"x": x, "y": y, "z": z}
                place[axis] = target(place[axis])
                pairs.append(
                    ((y * NZ + z) * NX + x, (place["y"] * NZ + place["z"]) * NX + place["x"])
                )
    return lax.ppermute(value, "dom", pairs)


def ahead(value, axis, step, size):
    return move(value, axis, lambda place: (place + step) % size)


def across(value, axis, flip):
    return move(value, axis, lambda place: place ^ flip)


def add_pairs(values):
    while len(values) > 1:
        values = [a + b for a, b in zip(values[::2], values[1::2])]
    return values[0]


def swap_shares(packed):
    groups = [
        [(y * NZ + z) * NX + x for z in range(NZ)] for y in range(NY) for x in range(NX)
    ]
    shares = packed.reshape(NZ, -1, packed.shape[1])
    return lax.all_to_all(
        shares, "dom", split_axis=0, concat_axis=0, tiled=True, axis_index_groups=groups
    )


def sum_along(mine, axis):
    return add_pairs([mine] + [across(mine, axis, flip) for flip in (1, 2, 3)])


def finish(ids, mine, grad_feats, classes, units):
    part, half = mine.shape
    got = [mine] + [ahead(mine, "z", d, NZ) for d in range(1, NZ)]
    got, grad_feats = lax.optimization_barrier((got, grad_feats))
    class_rows = -(-classes // 16) * 16

    def body(ids, *refs):
        shares, (out_w, out_c, out_b, packed) = refs[:NZ], refs[NZ:]
        for d, share in enumerate(shares):
            start = pl.multiple_of(lax.rem(ids[1] + NZ - d, NZ) * part, part)
            packed[pl.ds(start, part), :] = share[...]
        for k in range(units // half):
            out_w[:, k * half : (k + 1) * half] = packed[pl.ds(k * half, half), :].T
        out_c[...] = packed[pl.ds(units, classes), :]
        for k in range(units // half):
            row = units + class_rows + 8 * k
            out_b[:, k * half : (k + 1) * half] = packed[pl.ds(row, 1), :]

    grad_weight, grad_cls, grad_bias = pl.pallas_call(
        body,
        out_shape=(
            jax.ShapeDtypeStruct((half, units), F32),
            jax.ShapeDtypeStruct((classes, half), F32),
            jax.ShapeDtypeStruct((1, units), F32),
        ),
        in_specs=[SMEM] + [VMEM] * NZ,
        out_specs=(VMEM,) * 3,
        scratch_shapes=[pltpu.VMEM((PACKED, half), F32)],
        compiler_params=pltpu.CompilerParams(vmem_limit_bytes=4 * MIB),
        name="finish",
    )(ids, *got)
    return grad_feats, grad_weight, grad_bias[0], grad_cls.T


def on_device(feats, adj_tiles, adj_cols, send_rows, weight, bias, cls_w, labels):
    row_count, half = feats.shape
    tile = adj_tiles.shape[1]
    blocks = adj_cols.shape[0]
    peers, cap = send_rows.shape
    classes = cls_w.shape[1]
    units = weight.shape[1]
    total_nodes = row_count * lax.axis_size("dom")
    swap = [(0, 1), (1, 0)]

    rows = send_rows.T
    outgoing = gather_rows(rows, feats).reshape(peers, cap, half)
    incoming = lax.all_to_all(outgoing, "dom", split_axis=0, concat_axis=0, tiled=True)

    weight, cls_w, bias, labels, adj_cols, _ = lax.optimization_barrier(
        (weight, cls_w, bias, labels, adj_cols, outgoing)
    )
    cols = adj_cols.T
    dom = lax.axis_index("dom")
    ids = jnp.stack([lax.axis_index("hid"), dom // NX % NZ]).astype(jnp.int32)
    class_t = jnp.pad(cls_w.T, ((0, -classes % 16), (0, 0)))
    weight_o = lax.ppermute(weight, "hid", swap)
    class_o = lax.ppermute(class_t, "hid", swap)
    bias_row = bias[None, :]
    label_rows = labels.reshape(row_count // SPAN, SPAN)
    incoming, cols, ids, weight, weight_o, class_t, class_o, bias_row, label_rows = (
        lax.optimization_barrier(
            (incoming, cols, ids, weight, weight_o, class_t, class_o, bias_row, label_rows)
        )
    )

    halo = incoming.reshape(blocks, tile, half)
    agg = aggregate_blocks(cols, feats.reshape(blocks, tile, half), halo, adj_tiles)
    agg = agg.reshape(row_count, half)
    other = lax.ppermute(agg, "hid", swap)
    grads, packed = dense(
        ids, agg, other, weight, weight_o, class_t, class_o, bias_row, label_rows,
        classes, total_nodes,
    )
    halo_grad, own_grad = spread_blocks(cols, grads, adj_tiles)
    shares = swap_shares(packed)
    halo_grad, own_grad, shares = lax.optimization_barrier((halo_grad, own_grad, shares))
    returned = halo_grad.reshape(peers, cap, half)
    arrived = lax.all_to_all(returned, "dom", split_axis=0, concat_axis=0, tiled=True)
    share = sum_along(shares.sum(0), "x")
    own = jnp.swapaxes(own_grad, 1, 2).reshape(row_count, half)
    share, own = lax.optimization_barrier((share, own))
    share = sum_along(share, "y")
    grad_feats = scatter_rows(rows, arrived.reshape(row_count, half), own)
    return finish(ids, share, grad_feats, classes, units)


def solution(mesh):
    return jax.shard_map(
        on_device,
        mesh=mesh,
        in_specs=(
            P("dom", "hid"),
            P("dom", None, None),
            P("dom", None),
            P("dom", None),
            P("hid", None),
            P(),
            P("hid", None),
            P("dom"),
        ),
        out_specs=(P("dom", "hid"), P("hid", None), P(), P("hid", None)),
        check_vma=False,
    )
```

```python
import jax
import jax.numpy as jnp
from jax import lax
from jax.experimental import pallas as pl
from jax.experimental.pallas import tpu as pltpu
from jax.sharding import PartitionSpec as P

F32 = jnp.float32
BF16 = jnp.bfloat16
MIB = 1 << 20
VMEM = pl.BlockSpec(memory_space=pltpu.VMEM)
SMEM = pl.BlockSpec(memory_space=pltpu.SMEM)
HBM = pl.BlockSpec(memory_space=pltpu.HBM)
NX, NY, NZ = 4, 4, 8
PACKED = 448
TILE_STEPS = 4
SPAN = 4096


def contract(a, b, da, db):
    return lax.dot_general(a, b, (((da,), (db,)), ((), ())), preferred_element_type=F32)


def in_hbm(value):
    return pltpu.with_memory_space_constraint(value, pltpu.HBM)


def gather_kernel(rows_hbm, feats_hbm, out, rows, feats, table, picked, ready, row_sem, sems, out_sems):
    cap, peers = rows.shape
    count = feats.shape[0]
    part = count // sems.shape[0]
    some = peers // out_sems.shape[0]

    def part_copy(i):
        span = pl.ds(i * part, part)
        return pltpu.make_async_copy(feats_hbm.at[span], feats.at[span], sems.at[i])

    def out_copy(i):
        span = pl.ds(i * some * cap, some * cap)
        return pltpu.make_async_copy(ready.at[span], out.at[span], out_sems.at[i])

    row_copy = pltpu.make_async_copy(rows_hbm, rows, row_sem)
    row_copy.start()
    for i in range(sems.shape[0]):
        part_copy(i).start()
    table[pl.ds(count, 8), :] = jnp.zeros((8, table.shape[1]), F32)
    for i in range(sems.shape[0]):
        span = pl.ds(i * part, part)
        part_copy(i).wait()
        table[span, :] = feats[span, :].astype(F32)
    row_copy.wait()

    def one_peer(p, carry):
        base = pl.multiple_of(p * cap, cap)
        for c in range(cap):
            picked[pl.ds(base + c, 1), :] = table[pl.ds(rows[c, p], 1), :]
        return carry

    for i in range(out_sems.shape[0]):
        lax.fori_loop(i * some, (i + 1) * some, one_peer, 0)
        span = pl.ds(i * some * cap, some * cap)
        ready[span, :] = picked[span, :].astype(BF16)
        out_copy(i).start()
    for i in range(out_sems.shape[0]):
        out_copy(i).wait()


def gather_rows(rows, feats):
    count, width = feats.shape
    slots = rows.size
    return pl.pallas_call(
        gather_kernel,
        out_shape=pltpu.HBM((slots, width), BF16),
        in_specs=[HBM, HBM],
        out_specs=HBM,
        scratch_shapes=[
            pltpu.SMEM(rows.shape, rows.dtype),
            pltpu.VMEM(feats.shape, BF16),
            pltpu.VMEM((count + 8, width), F32),
            pltpu.VMEM((slots, width), F32),
            pltpu.VMEM((slots, width), BF16),
            pltpu.SemaphoreType.DMA,
            pltpu.SemaphoreType.DMA((4,)),
            pltpu.SemaphoreType.DMA((4,)),
        ],
        compiler_params=pltpu.CompilerParams(vmem_limit_bytes=12 * MIB),
        cost_estimate=pl.CostEstimate(flops=0, bytes_accessed=8 * MIB, transcendentals=0),
        name="gather_rows",
    )(in_hbm(rows), in_hbm(feats))


def tile_copy(adj, tiles, sems, i):
    span = pl.ds(i * (adj.shape[0] // sems.shape[0]), adj.shape[0] // sems.shape[0])
    return pltpu.make_async_copy(adj.at[span], tiles.at[span], sems.at[i])


def aggregate_kernel(cols, feats, halo, adj, agg, ext, tiles, sems):
    nonzero, blocks = cols.shape
    steps = sems.shape[0]
    per_step = blocks // steps
    for i in range(steps):
        tile_copy(adj, tiles, sems, i).start()
    ext[pl.ds(0, blocks)] = feats[...]
    ext[pl.ds(blocks, halo.shape[0])] = halo[...]

    def one_step(i, carry):
        tile_copy(adj, tiles, sems, i).wait()
        for j in range(per_step):
            r = i * per_step + j
            left = jnp.concatenate([tiles[r * nonzero + k] for k in range(nonzero)], 1)
            right = jnp.concatenate([ext[cols[k, r]] for k in range(nonzero)], 0)
            agg[r] = contract(left, right, 1, 0).astype(BF16)
        return carry

    lax.fori_loop(0, steps, one_step, 0)


def aggregate_blocks(cols, feats, halo, adj):
    return pl.pallas_call(
        aggregate_kernel,
        out_shape=jax.ShapeDtypeStruct(feats.shape, BF16),
        in_specs=[SMEM, VMEM, VMEM, HBM],
        out_specs=VMEM,
        scratch_shapes=[
            pltpu.VMEM((feats.shape[0] + halo.shape[0],) + feats.shape[1:], BF16),
            pltpu.VMEM(adj.shape, BF16),
            pltpu.SemaphoreType.DMA((TILE_STEPS,)),
        ],
        compiler_params=pltpu.CompilerParams(vmem_limit_bytes=24 * MIB),
        cost_estimate=pl.CostEstimate(flops=1 << 30, bytes_accessed=12 * MIB, transcendentals=0),
        name="aggregate_blocks",
    )(cols, feats, halo, in_hbm(adj))


def dense_kernel(
    classes, total_nodes, ids, agg, other, weight, weight_o, class_t, class_o, bias_row, labels,
    grad_out, packed,
    sum_w, sum_c, sum_b, weight_t, cls_t, cls, bias,
):
    steps = labels.shape[0]
    class_rows = cls_t.shape[0]
    first = ids[0] == 0
    half = agg.shape[1]

    def both(mine, theirs, dim):
        return jnp.concatenate(
            [jnp.where(first, mine, theirs), jnp.where(first, theirs, mine)], dim
        )

    weight_t[...] = both(weight[...], weight_o[...], 0).T
    cls_t[...] = both(class_t[...], class_o[...], 1)
    cls[...] = cls_t[...].T
    bias[...] = jnp.broadcast_to(bias_row[...], (128, 2 * half)).T
    sum_w[...] = jnp.zeros_like(sum_w)
    sum_c[...] = jnp.zeros_like(sum_c)
    sum_b[...] = jnp.zeros_like(sum_b)
    class_id = lax.broadcasted_iota(jnp.int32, (class_rows, SPAN), 0)

    def one_step(i, carry):
        nodes = pl.ds(pl.multiple_of(i * SPAN, SPAN), SPAN)
        mine = agg[nodes, :]
        preact = contract(weight_t[...], both(mine, other[nodes, :], 1), 1, 1)
        preact = preact + jnp.tile(bias[...], (1, SPAN // bias.shape[1]))
        hidden = jnp.maximum(preact, 0.0).astype(BF16)
        logits = contract(cls_t[...], hidden, 1, 0)
        logits = jnp.where(class_id < classes, logits, -jnp.inf)
        powers = jnp.exp(logits - jnp.max(logits, 0, keepdims=True))
        share = powers * (1.0 / jnp.sum(powers, 0, keepdims=True))
        label = labels[pl.ds(i, 1), :]
        logit_grad = (share - jnp.where(class_id == label, 1.0, 0.0)).astype(BF16)
        hidden_grad = contract(cls[...], logit_grad, 1, 0)
        preact_grad = jnp.where(preact > 0, hidden_grad, 0.0).astype(BF16)
        own_hidden = jnp.where(first, hidden[:half], hidden[half:])
        sum_w[...] += contract(preact_grad, mine, 1, 0)
        sum_c[...] += contract(logit_grad, own_hidden, 1, 1)
        sum_b[...] += contract(jnp.ones((8, SPAN), BF16), preact_grad, 1, 1)
        agg_grad = contract(weight[...], preact_grad, 1, 0).astype(BF16)
        for j in range(SPAN // half):
            grad_out[i * (SPAN // half) + j] = agg_grad[:, j * half : (j + 1) * half]
        return carry

    lax.fori_loop(0, steps, one_step, 0)
    scale = 1.0 / total_nodes
    units = 2 * half
    packed[pl.ds(0, units), :] = sum_w[...] * scale
    packed[pl.ds(units, class_rows), :] = sum_c[...] * scale
    packed[pl.ds(units + class_rows, 8), :] = sum_b[:, :half] * scale
    packed[pl.ds(units + class_rows + 8, 8), :] = sum_b[:, half:] * scale


def dense(ids, agg, other, weight, weight_o, class_t, class_o, bias_row, labels, classes, total_nodes):
    rows, half = agg.shape
    units = weight.shape[1]
    steps = rows // SPAN
    class_rows = class_t.shape[0]

    def body(*refs):
        dense_kernel(classes, total_nodes, *refs)

    return pl.pallas_call(
        body,
        out_shape=(
            jax.ShapeDtypeStruct((rows // half, half, half), BF16),
            jax.ShapeDtypeStruct((PACKED, half), F32),
        ),
        in_specs=[SMEM] + [VMEM] * 8,
        out_specs=(VMEM,) * 2,
        scratch_shapes=[
            pltpu.VMEM((units, half), F32),
            pltpu.VMEM((class_rows, half), F32),
            pltpu.VMEM((8, units), F32),
            pltpu.VMEM((units, 2 * half), BF16),
            pltpu.VMEM((class_rows, units), BF16),
            pltpu.VMEM((units, class_rows), BF16),
            pltpu.VMEM((units, 128), F32),
        ],
        compiler_params=pltpu.CompilerParams(vmem_limit_bytes=32 * MIB),
        cost_estimate=pl.CostEstimate(flops=5 << 30, bytes_accessed=4 * MIB, transcendentals=1 << 20),
        name="dense",
    )(ids, agg, other, weight, weight_o, class_t, class_o, bias_row, labels)


def spread_kernel(cols, grads, adj, halo_out, own_out, ext_grad, tiles, sems, own_sem):
    nonzero, blocks = cols.shape
    tile = adj.shape[1]
    steps = sems.shape[0]
    per_step = blocks // steps
    for i in range(steps):
        tile_copy(adj, tiles, sems, i).start()
    ext_grad[...] = jnp.zeros_like(ext_grad)

    def one_step(i, carry):
        tile_copy(adj, tiles, sems, i).wait()
        for j in range(per_step):
            r = i * per_step + j
            right = jnp.concatenate([tiles[r * nonzero + k] for k in range(nonzero)], 1)
            term = contract(grads[r], right, 1, 0)
            for k in range(nonzero):
                ext_grad[cols[k, r]] += term[:, k * tile : (k + 1) * tile]
        return carry

    lax.fori_loop(0, steps, one_step, 0)
    own_copy = pltpu.make_async_copy(ext_grad.at[pl.ds(0, blocks)], own_out, own_sem)
    own_copy.start()

    def one_halo(b, carry):
        halo_out[b] = ext_grad[blocks + b].T.astype(BF16)
        return carry

    lax.fori_loop(0, halo_out.shape[0], one_halo, 0, unroll=4)
    own_copy.wait()


def spread_blocks(cols, grads, adj):
    blocks = cols.shape[1]
    tile = adj.shape[1]
    half = grads.shape[1]
    return pl.pallas_call(
        spread_kernel,
        out_shape=(
            jax.ShapeDtypeStruct((blocks, tile, half), BF16),
            pltpu.HBM((blocks, half, tile), F32),
        ),
        in_specs=[SMEM, VMEM, HBM],
        out_specs=(VMEM, HBM),
        scratch_shapes=[
            pltpu.VMEM((2 * blocks, half, tile), F32),
            pltpu.VMEM(adj.shape, BF16),
            pltpu.SemaphoreType.DMA((TILE_STEPS,)),
            pltpu.SemaphoreType.DMA,
        ],
        compiler_params=pltpu.CompilerParams(vmem_limit_bytes=24 * MIB),
        cost_estimate=pl.CostEstimate(flops=1 << 30, bytes_accessed=12 * MIB, transcendentals=0),
        name="spread_blocks",
    )(cols, grads, in_hbm(adj))


def scatter_kernel(rows_hbm, arrived, own, out, rows, values, ready, row_sem, out_sems, *sums):
    cap, peers = rows.shape
    count, width = out.shape
    row_copy = pltpu.make_async_copy(rows_hbm, rows, row_sem)
    row_copy.start()
    values[...] = arrived[...].astype(F32)
    sums[0][pl.ds(0, count), :] = own[...]
    for total in sums[1:]:
        total[...] = jnp.zeros_like(total)
    row_copy.wait()

    def one_peer(p, carry):
        base = pl.multiple_of(p * cap, cap)
        for c in range(cap):
            total = sums[c % len(sums)]
            row = pl.ds(rows[c, p], 1)
            total[row, :] = total[row, :] + values[pl.ds(base + c, 1), :]
        return carry

    lax.fori_loop(0, peers, one_peer, 0)
    part = count // out_sems.shape[0]

    def out_copy(i):
        span = pl.ds(i * part, part)
        return pltpu.make_async_copy(ready.at[span], out.at[span], out_sems.at[i])

    for i in range(out_sems.shape[0]):
        span = pl.ds(i * part, part)
        result = sums[0][span, :]
        for total in sums[1:]:
            result = result + total[span, :]
        ready[span, :] = result.astype(BF16)
        out_copy(i).start()
    for i in range(out_sems.shape[0]):
        out_copy(i).wait()


def scatter_rows(rows, arrived, own):
    count, width = own.shape
    lanes = 8
    return pl.pallas_call(
        scatter_kernel,
        out_shape=pltpu.HBM((count, width), BF16),
        in_specs=[HBM, VMEM, VMEM],
        out_specs=HBM,
        scratch_shapes=[
            pltpu.SMEM(rows.shape, rows.dtype),
            pltpu.VMEM(arrived.shape, F32),
            pltpu.VMEM((count, width), BF16),
            pltpu.SemaphoreType.DMA,
            pltpu.SemaphoreType.DMA((4,)),
        ]
        + [pltpu.VMEM((count + 8, width), F32)] * lanes,
        compiler_params=pltpu.CompilerParams(vmem_limit_bytes=32 * MIB),
        cost_estimate=pl.CostEstimate(flops=0, bytes_accessed=8 * MIB, transcendentals=0),
        name="scatter_rows",
    )(in_hbm(rows), arrived, own)


def move(value, axis, target):
    pairs = []
    for y in range(NY):
        for z in range(NZ):
            for x in range(NX):
                place = {"x": x, "y": y, "z": z}
                place[axis] = target(place[axis])
                pairs.append(
                    ((y * NZ + z) * NX + x, (place["y"] * NZ + place["z"]) * NX + place["x"])
                )
    return lax.ppermute(value, "dom", pairs)


def ahead(value, axis, step, size):
    return move(value, axis, lambda place: (place + step) % size)


def across(value, axis, flip):
    return move(value, axis, lambda place: place ^ flip)


def add_pairs(values):
    while len(values) > 1:
        values = [a + b for a, b in zip(values[::2], values[1::2])]
    return values[0]


def swap_shares(packed):
    groups = [
        [(y * NZ + z) * NX + x for z in range(NZ)] for y in range(NY) for x in range(NX)
    ]
    shares = packed.reshape(NZ, -1, packed.shape[1])
    return lax.all_to_all(
        shares, "dom", split_axis=0, concat_axis=0, tiled=True, axis_index_groups=groups
    )


def sum_along(mine, axis):
    return add_pairs([mine] + [across(mine, axis, flip) for flip in (1, 2, 3)])


def finish(ids, mine, grad_feats, classes, units):
    part, half = mine.shape
    got = [mine] + [ahead(mine, "z", d, NZ) for d in range(1, NZ)]
    got, grad_feats = lax.optimization_barrier((got, grad_feats))
    class_rows = -(-classes // 16) * 16

    def body(ids, *refs):
        shares, (out_w, out_c, out_b, packed) = refs[:NZ], refs[NZ:]
        for d, share in enumerate(shares):
            start = pl.multiple_of(lax.rem(ids[1] + NZ - d, NZ) * part, part)
            packed[pl.ds(start, part), :] = share[...]
        for k in range(units // half):
            out_w[:, k * half : (k + 1) * half] = packed[pl.ds(k * half, half), :].T
        out_c[...] = packed[pl.ds(units, classes), :]
        for k in range(units // half):
            row = units + class_rows + 8 * k
            out_b[:, k * half : (k + 1) * half] = packed[pl.ds(row, 1), :]

    grad_weight, grad_cls, grad_bias = pl.pallas_call(
        body,
        out_shape=(
            jax.ShapeDtypeStruct((half, units), F32),
            jax.ShapeDtypeStruct((classes, half), F32),
            jax.ShapeDtypeStruct((1, units), F32),
        ),
        in_specs=[SMEM] + [VMEM] * NZ,
        out_specs=(VMEM,) * 3,
        scratch_shapes=[pltpu.VMEM((PACKED, half), F32)],
        compiler_params=pltpu.CompilerParams(vmem_limit_bytes=4 * MIB),
        name="finish",
    )(ids, *got)
    return grad_feats, grad_weight, grad_bias[0], grad_cls.T


def on_device(feats, adj_tiles, adj_cols, send_rows, weight, bias, cls_w, labels):
    row_count, half = feats.shape
    tile = adj_tiles.shape[1]
    blocks = adj_cols.shape[0]
    peers, cap = send_rows.shape
    classes = cls_w.shape[1]
    units = weight.shape[1]
    total_nodes = row_count * lax.axis_size("dom")
    swap = [(0, 1), (1, 0)]

    rows = send_rows.T
    outgoing = gather_rows(rows, feats).reshape(peers, cap, half)
    incoming = lax.all_to_all(outgoing, "dom", split_axis=0, concat_axis=0, tiled=True)

    weight, cls_w, bias, labels, adj_cols, _ = lax.optimization_barrier(
        (weight, cls_w, bias, labels, adj_cols, outgoing)
    )
    cols = adj_cols.T
    dom = lax.axis_index("dom")
    ids = jnp.stack([lax.axis_index("hid"), dom // NX % NZ]).astype(jnp.int32)
    class_t = jnp.pad(cls_w.T, ((0, -classes % 16), (0, 0)))
    weight_o = lax.ppermute(weight, "hid", swap)
    class_o = lax.ppermute(class_t, "hid", swap)
    bias_row = bias[None, :]
    label_rows = labels.reshape(row_count // SPAN, SPAN)
    incoming, cols, ids, weight, weight_o, class_t, class_o, bias_row, label_rows = (
        lax.optimization_barrier(
            (incoming, cols, ids, weight, weight_o, class_t, class_o, bias_row, label_rows)
        )
    )

    halo = incoming.reshape(blocks, tile, half)
    agg = aggregate_blocks(cols, feats.reshape(blocks, tile, half), halo, adj_tiles)
    agg = agg.reshape(row_count, half)
    other = lax.ppermute(agg, "hid", swap)
    grads, packed = dense(
        ids, agg, other, weight, weight_o, class_t, class_o, bias_row, label_rows,
        classes, total_nodes,
    )
    halo_grad, own_grad = spread_blocks(cols, grads, adj_tiles)
    shares = swap_shares(packed)
    halo_grad, own_grad, shares = lax.optimization_barrier((halo_grad, own_grad, shares))
    returned = halo_grad.reshape(peers, cap, half)
    arrived = lax.all_to_all(returned, "dom", split_axis=0, concat_axis=0, tiled=True)
    share = sum_along(shares.sum(0), "x")
    own = jnp.swapaxes(own_grad, 1, 2).reshape(row_count, half)
    share, own = lax.optimization_barrier((share, own))
    share = sum_along(share, "y")
    grad_feats = scatter_rows(rows, arrived.reshape(row_count, half), own)
    return finish(ids, share, grad_feats, classes, units)


def solution(mesh):
    return jax.shard_map(
        on_device,
        mesh=mesh,
        in_specs=(
            P("dom", "hid"),
            P("dom", None, None),
            P("dom", None),
            P("dom", None),
            P("hid", None),
            P(),
            P("hid", None),
            P("dom"),
        ),
        out_specs=(P("dom", "hid"), P("hid", None), P(), P("hid", None)),
        check_vma=False,
    )
```

```python
import jax
import jax.numpy as jnp
from jax import lax
from jax.experimental import pallas as pl
from jax.experimental.pallas import tpu as pltpu
from jax.sharding import PartitionSpec as P

F32 = jnp.float32
BF16 = jnp.bfloat16
MIB = 1 << 20
VMEM = pl.BlockSpec(memory_space=pltpu.VMEM)
SMEM = pl.BlockSpec(memory_space=pltpu.SMEM)
HBM = pl.BlockSpec(memory_space=pltpu.HBM)
NX, NY, NZ = 4, 4, 8
PACKED = 448
TILE_STEPS = 4
SPAN = 4096


def contract(a, b, da, db):
    return lax.dot_general(a, b, (((da,), (db,)), ((), ())), preferred_element_type=F32)


def in_hbm(value):
    return pltpu.with_memory_space_constraint(value, pltpu.HBM)


def gather_kernel(rows_hbm, feats_hbm, out, rows, feats, table, picked, ready, row_sem, sems, out_sems):
    cap, peers = rows.shape
    count = feats.shape[0]
    part = count // sems.shape[0]
    some = peers // out_sems.shape[0]

    def part_copy(i):
        span = pl.ds(i * part, part)
        return pltpu.make_async_copy(feats_hbm.at[span], feats.at[span], sems.at[i])

    def out_copy(i):
        span = pl.ds(i * some * cap, some * cap)
        return pltpu.make_async_copy(ready.at[span], out.at[span], out_sems.at[i])

    row_copy = pltpu.make_async_copy(rows_hbm, rows, row_sem)
    row_copy.start()
    for i in range(sems.shape[0]):
        part_copy(i).start()
    table[pl.ds(count, 8), :] = jnp.zeros((8, table.shape[1]), F32)
    for i in range(sems.shape[0]):
        span = pl.ds(i * part, part)
        part_copy(i).wait()
        table[span, :] = feats[span, :].astype(F32)
    row_copy.wait()

    def one_peer(p, carry):
        base = pl.multiple_of(p * cap, cap)
        for c in range(cap):
            picked[pl.ds(base + c, 1), :] = table[pl.ds(rows[c, p], 1), :]
        return carry

    for i in range(out_sems.shape[0]):
        lax.fori_loop(i * some, (i + 1) * some, one_peer, 0)
        span = pl.ds(i * some * cap, some * cap)
        ready[span, :] = picked[span, :].astype(BF16)
        out_copy(i).start()
    for i in range(out_sems.shape[0]):
        out_copy(i).wait()


def gather_rows(rows, feats):
    count, width = feats.shape
    slots = rows.size
    return pl.pallas_call(
        gather_kernel,
        out_shape=pltpu.HBM((slots, width), BF16),
        in_specs=[HBM, HBM],
        out_specs=HBM,
        scratch_shapes=[
            pltpu.SMEM(rows.shape, rows.dtype),
            pltpu.VMEM(feats.shape, BF16),
            pltpu.VMEM((count + 8, width), F32),
            pltpu.VMEM((slots, width), F32),
            pltpu.VMEM((slots, width), BF16),
            pltpu.SemaphoreType.DMA,
            pltpu.SemaphoreType.DMA((4,)),
            pltpu.SemaphoreType.DMA((4,)),
        ],
        compiler_params=pltpu.CompilerParams(vmem_limit_bytes=12 * MIB),
        cost_estimate=pl.CostEstimate(flops=0, bytes_accessed=8 * MIB, transcendentals=0),
        name="gather_rows",
    )(in_hbm(rows), in_hbm(feats))


def tile_copy(adj, tiles, sems, i):
    span = pl.ds(i * (adj.shape[0] // sems.shape[0]), adj.shape[0] // sems.shape[0])
    return pltpu.make_async_copy(adj.at[span], tiles.at[span], sems.at[i])


def aggregate_kernel(cols, feats, halo, adj, agg, ext, tiles, sems):
    nonzero, blocks = cols.shape
    steps = sems.shape[0]
    per_step = blocks // steps
    for i in range(steps):
        tile_copy(adj, tiles, sems, i).start()
    ext[pl.ds(0, blocks)] = feats[...]
    ext[pl.ds(blocks, halo.shape[0])] = halo[...]

    def one_step(i, carry):
        tile_copy(adj, tiles, sems, i).wait()
        for j in range(per_step):
            r = i * per_step + j
            left = jnp.concatenate([tiles[r * nonzero + k] for k in range(nonzero)], 1)
            right = jnp.concatenate([ext[cols[k, r]] for k in range(nonzero)], 0)
            agg[r] = contract(left, right, 1, 0).astype(BF16)
        return carry

    lax.fori_loop(0, steps, one_step, 0)


def aggregate_blocks(cols, feats, halo, adj):
    return pl.pallas_call(
        aggregate_kernel,
        out_shape=jax.ShapeDtypeStruct(feats.shape, BF16),
        in_specs=[SMEM, VMEM, VMEM, HBM],
        out_specs=VMEM,
        scratch_shapes=[
            pltpu.VMEM((feats.shape[0] + halo.shape[0],) + feats.shape[1:], BF16),
            pltpu.VMEM(adj.shape, BF16),
            pltpu.SemaphoreType.DMA((TILE_STEPS,)),
        ],
        compiler_params=pltpu.CompilerParams(vmem_limit_bytes=24 * MIB),
        cost_estimate=pl.CostEstimate(flops=1 << 30, bytes_accessed=12 * MIB, transcendentals=0),
        name="aggregate_blocks",
    )(cols, feats, halo, in_hbm(adj))


def dense_kernel(
    classes, total_nodes, ids, agg, other, weight, weight_o, class_t, class_o, bias_row, labels,
    grad_out, packed,
    sum_w, sum_c, sum_b, weight_t, cls_t, cls, bias,
):
    steps = labels.shape[0]
    class_rows = cls_t.shape[0]
    first = ids[0] == 0
    half = agg.shape[1]

    def both(mine, theirs, dim):
        return jnp.concatenate(
            [jnp.where(first, mine, theirs), jnp.where(first, theirs, mine)], dim
        )

    weight_t[...] = both(weight[...], weight_o[...], 0).T
    cls_t[...] = both(class_t[...], class_o[...], 1)
    cls[...] = cls_t[...].T
    bias[...] = jnp.broadcast_to(bias_row[...], (128, 2 * half)).T
    sum_w[...] = jnp.zeros_like(sum_w)
    sum_c[...] = jnp.zeros_like(sum_c)
    sum_b[...] = jnp.zeros_like(sum_b)
    class_id = lax.broadcasted_iota(jnp.int32, (class_rows, SPAN), 0)
    class_full = classes // 8 * 8

    def one_step(i, carry):
        nodes = pl.ds(pl.multiple_of(i * SPAN, SPAN), SPAN)
        mine = agg[nodes, :]
        preact = contract(weight_t[...], both(mine, other[nodes, :], 1), 1, 1)
        preact = preact + jnp.tile(bias[...], (1, SPAN // bias.shape[1]))
        hidden = jnp.maximum(preact, 0.0).astype(BF16)
        logits = contract(cls_t[...], hidden, 1, 0)
        tail = jnp.where(class_id[class_full:] < classes, logits[class_full:], -jnp.inf)
        logits = jnp.concatenate([logits[:class_full], tail], 0)
        powers = jnp.exp(logits - jnp.max(logits, 0, keepdims=True))
        share = powers * (1.0 / jnp.sum(powers, 0, keepdims=True))
        label = labels[pl.ds(i, 1), :]
        logit_grad = (share - jnp.where(class_id == label, 1.0, 0.0)).astype(BF16)
        hidden_grad = contract(cls[...], logit_grad, 1, 0)
        preact_grad = jnp.where(preact > 0, hidden_grad, 0.0).astype(BF16)
        own_hidden = jnp.where(first, hidden[:half], hidden[half:])
        sum_w[...] += contract(preact_grad, mine, 1, 0)
        sum_c[...] += contract(logit_grad, own_hidden, 1, 1)
        sum_b[...] += contract(jnp.ones((8, SPAN), BF16), preact_grad, 1, 1)
        agg_grad = contract(weight[...], preact_grad, 1, 0).astype(BF16)
        for j in range(SPAN // half):
            grad_out[i * (SPAN // half) + j] = agg_grad[:, j * half : (j + 1) * half]
        return carry

    lax.fori_loop(0, steps, one_step, 0)
    scale = 1.0 / total_nodes
    units = 2 * half
    packed[pl.ds(0, units), :] = sum_w[...] * scale
    packed[pl.ds(units, class_rows), :] = sum_c[...] * scale
    packed[pl.ds(units + class_rows, 8), :] = sum_b[:, :half] * scale
    packed[pl.ds(units + class_rows + 8, 8), :] = sum_b[:, half:] * scale


def dense(ids, agg, other, weight, weight_o, class_t, class_o, bias_row, labels, classes, total_nodes):
    rows, half = agg.shape
    units = weight.shape[1]
    steps = rows // SPAN
    class_rows = class_t.shape[0]

    def body(*refs):
        dense_kernel(classes, total_nodes, *refs)

    return pl.pallas_call(
        body,
        out_shape=(
            jax.ShapeDtypeStruct((rows // half, half, half), BF16),
            jax.ShapeDtypeStruct((PACKED, half), F32),
        ),
        in_specs=[SMEM] + [VMEM] * 8,
        out_specs=(VMEM,) * 2,
        scratch_shapes=[
            pltpu.VMEM((units, half), F32),
            pltpu.VMEM((class_rows, half), F32),
            pltpu.VMEM((8, units), F32),
            pltpu.VMEM((units, 2 * half), BF16),
            pltpu.VMEM((class_rows, units), BF16),
            pltpu.VMEM((units, class_rows), BF16),
            pltpu.VMEM((units, 128), F32),
        ],
        compiler_params=pltpu.CompilerParams(vmem_limit_bytes=32 * MIB),
        cost_estimate=pl.CostEstimate(flops=5 << 30, bytes_accessed=4 * MIB, transcendentals=1 << 20),
        name="dense",
    )(ids, agg, other, weight, weight_o, class_t, class_o, bias_row, labels)


def spread_kernel(cols, grads, adj, halo_out, own_out, ext_grad, tiles, sems, own_sem):
    nonzero, blocks = cols.shape
    tile = adj.shape[1]
    steps = sems.shape[0]
    per_step = blocks // steps
    for i in range(steps):
        tile_copy(adj, tiles, sems, i).start()
    ext_grad[...] = jnp.zeros_like(ext_grad)

    def one_step(i, carry):
        tile_copy(adj, tiles, sems, i).wait()
        for j in range(per_step):
            r = i * per_step + j
            right = jnp.concatenate([tiles[r * nonzero + k] for k in range(nonzero)], 1)
            term = contract(grads[r], right, 1, 0)
            for k in range(nonzero):
                ext_grad[cols[k, r]] += term[:, k * tile : (k + 1) * tile]
        return carry

    lax.fori_loop(0, steps, one_step, 0)
    own_copy = pltpu.make_async_copy(ext_grad.at[pl.ds(0, blocks)], own_out, own_sem)
    own_copy.start()

    def one_halo(b, carry):
        halo_out[b] = ext_grad[blocks + b].T.astype(BF16)
        return carry

    lax.fori_loop(0, halo_out.shape[0], one_halo, 0, unroll=4)
    own_copy.wait()


def spread_blocks(cols, grads, adj):
    blocks = cols.shape[1]
    tile = adj.shape[1]
    half = grads.shape[1]
    return pl.pallas_call(
        spread_kernel,
        out_shape=(
            jax.ShapeDtypeStruct((blocks, tile, half), BF16),
            pltpu.HBM((blocks, half, tile), F32),
        ),
        in_specs=[SMEM, VMEM, HBM],
        out_specs=(VMEM, HBM),
        scratch_shapes=[
            pltpu.VMEM((2 * blocks, half, tile), F32),
            pltpu.VMEM(adj.shape, BF16),
            pltpu.SemaphoreType.DMA((TILE_STEPS,)),
            pltpu.SemaphoreType.DMA,
        ],
        compiler_params=pltpu.CompilerParams(vmem_limit_bytes=24 * MIB),
        cost_estimate=pl.CostEstimate(flops=1 << 30, bytes_accessed=12 * MIB, transcendentals=0),
        name="spread_blocks",
    )(cols, grads, in_hbm(adj))


def scatter_kernel(rows_hbm, arrived, own, out, rows, values, ready, row_sem, out_sems, *sums):
    cap, peers = rows.shape
    count, width = out.shape
    row_copy = pltpu.make_async_copy(rows_hbm, rows, row_sem)
    row_copy.start()
    values[...] = arrived[...].astype(F32)
    sums[0][pl.ds(0, count), :] = own[...]
    for total in sums[1:]:
        total[...] = jnp.zeros_like(total)
    row_copy.wait()

    def one_peer(p, carry):
        base = pl.multiple_of(p * cap, cap)
        for c in range(cap):
            total = sums[c % len(sums)]
            row = pl.ds(rows[c, p], 1)
            total[row, :] = total[row, :] + values[pl.ds(base + c, 1), :]
        return carry

    lax.fori_loop(0, peers, one_peer, 0)
    part = count // out_sems.shape[0]

    def out_copy(i):
        span = pl.ds(i * part, part)
        return pltpu.make_async_copy(ready.at[span], out.at[span], out_sems.at[i])

    for i in range(out_sems.shape[0]):
        span = pl.ds(i * part, part)
        result = sums[0][span, :]
        for total in sums[1:]:
            result = result + total[span, :]
        ready[span, :] = result.astype(BF16)
        out_copy(i).start()
    for i in range(out_sems.shape[0]):
        out_copy(i).wait()


def scatter_rows(rows, arrived, own):
    count, width = own.shape
    lanes = 6
    return pl.pallas_call(
        scatter_kernel,
        out_shape=pltpu.HBM((count, width), BF16),
        in_specs=[HBM, VMEM, VMEM],
        out_specs=HBM,
        scratch_shapes=[
            pltpu.SMEM(rows.shape, rows.dtype),
            pltpu.VMEM(arrived.shape, F32),
            pltpu.VMEM((count, width), BF16),
            pltpu.SemaphoreType.DMA,
            pltpu.SemaphoreType.DMA((4,)),
        ]
        + [pltpu.VMEM((count + 8, width), F32)] * lanes,
        compiler_params=pltpu.CompilerParams(vmem_limit_bytes=32 * MIB),
        cost_estimate=pl.CostEstimate(flops=0, bytes_accessed=8 * MIB, transcendentals=0),
        name="scatter_rows",
    )(in_hbm(rows), arrived, own)


def move(value, axis, target):
    pairs = []
    for y in range(NY):
        for z in range(NZ):
            for x in range(NX):
                place = {"x": x, "y": y, "z": z}
                place[axis] = target(place[axis])
                pairs.append(
                    ((y * NZ + z) * NX + x, (place["y"] * NZ + place["z"]) * NX + place["x"])
                )
    return lax.ppermute(value, "dom", pairs)


def ahead(value, axis, step, size):
    return move(value, axis, lambda place: (place + step) % size)


def across(value, axis, flip):
    return move(value, axis, lambda place: place ^ flip)


def add_pairs(values):
    while len(values) > 1:
        values = [a + b for a, b in zip(values[::2], values[1::2])]
    return values[0]


def swap_shares(packed):
    groups = [
        [(y * NZ + z) * NX + x for z in range(NZ)] for y in range(NY) for x in range(NX)
    ]
    shares = packed.reshape(NZ, -1, packed.shape[1])
    return lax.all_to_all(
        shares, "dom", split_axis=0, concat_axis=0, tiled=True, axis_index_groups=groups
    )


def sum_along(mine, axis):
    return add_pairs([mine] + [across(mine, axis, flip) for flip in (1, 2, 3)])


def finish(ids, mine, grad_feats, classes, units):
    part, half = mine.shape
    got = [mine] + [ahead(mine, "z", d, NZ) for d in range(1, NZ)]
    got, grad_feats = lax.optimization_barrier((got, grad_feats))
    class_rows = -(-classes // 16) * 16

    def body(ids, *refs):
        shares, (out_w, out_c, out_b, packed) = refs[:NZ], refs[NZ:]
        for d, share in enumerate(shares):
            start = pl.multiple_of(lax.rem(ids[1] + NZ - d, NZ) * part, part)
            packed[pl.ds(start, part), :] = share[...]
        for k in range(units // half):
            out_w[:, k * half : (k + 1) * half] = packed[pl.ds(k * half, half), :].T
        out_c[...] = packed[pl.ds(units, classes), :]
        for k in range(units // half):
            row = units + class_rows + 8 * k
            out_b[:, k * half : (k + 1) * half] = packed[pl.ds(row, 1), :]

    grad_weight, grad_cls, grad_bias = pl.pallas_call(
        body,
        out_shape=(
            jax.ShapeDtypeStruct((half, units), F32),
            jax.ShapeDtypeStruct((classes, half), F32),
            jax.ShapeDtypeStruct((1, units), F32),
        ),
        in_specs=[SMEM] + [VMEM] * NZ,
        out_specs=(VMEM,) * 3,
        scratch_shapes=[pltpu.VMEM((PACKED, half), F32)],
        compiler_params=pltpu.CompilerParams(vmem_limit_bytes=4 * MIB),
        name="finish",
    )(ids, *got)
    return grad_feats, grad_weight, grad_bias[0], grad_cls.T


def on_device(feats, adj_tiles, adj_cols, send_rows, weight, bias, cls_w, labels):
    row_count, half = feats.shape
    tile = adj_tiles.shape[1]
    blocks = adj_cols.shape[0]
    peers, cap = send_rows.shape
    classes = cls_w.shape[1]
    units = weight.shape[1]
    total_nodes = row_count * lax.axis_size("dom")
    swap = [(0, 1), (1, 0)]

    rows = send_rows.T
    outgoing = gather_rows(rows, feats).reshape(peers, cap, half)
    incoming = lax.all_to_all(outgoing, "dom", split_axis=0, concat_axis=0, tiled=True)

    weight, cls_w, bias, labels, adj_cols, _ = lax.optimization_barrier(
        (weight, cls_w, bias, labels, adj_cols, outgoing)
    )
    cols = adj_cols.T
    dom = lax.axis_index("dom")
    ids = jnp.stack([lax.axis_index("hid"), dom // NX % NZ]).astype(jnp.int32)
    class_t = jnp.pad(cls_w.T, ((0, -classes % 16), (0, 0)))
    weight_o = lax.ppermute(weight, "hid", swap)
    class_o = lax.ppermute(class_t, "hid", swap)
    bias_row = bias[None, :]
    label_rows = labels.reshape(row_count // SPAN, SPAN)
    incoming, cols, ids, weight, weight_o, class_t, class_o, bias_row, label_rows = (
        lax.optimization_barrier(
            (incoming, cols, ids, weight, weight_o, class_t, class_o, bias_row, label_rows)
        )
    )

    halo = incoming.reshape(blocks, tile, half)
    agg = aggregate_blocks(cols, feats.reshape(blocks, tile, half), halo, adj_tiles)
    agg = agg.reshape(row_count, half)
    other = lax.ppermute(agg, "hid", swap)
    grads, packed = dense(
        ids, agg, other, weight, weight_o, class_t, class_o, bias_row, label_rows,
        classes, total_nodes,
    )
    halo_grad, own_grad = spread_blocks(cols, grads, adj_tiles)
    shares = swap_shares(packed)
    halo_grad, own_grad, shares = lax.optimization_barrier((halo_grad, own_grad, shares))
    returned = halo_grad.reshape(peers, cap, half)
    arrived = lax.all_to_all(returned, "dom", split_axis=0, concat_axis=0, tiled=True)
    share = sum_along(shares.sum(0), "x")
    own = jnp.swapaxes(own_grad, 1, 2).reshape(row_count, half)
    share, own = lax.optimization_barrier((share, own))
    share = sum_along(share, "y")
    grad_feats = scatter_rows(rows, arrived.reshape(row_count, half), own)
    return finish(ids, share, grad_feats, classes, units)


def solution(mesh):
    return jax.shard_map(
        on_device,
        mesh=mesh,
        in_specs=(
            P("dom", "hid"),
            P("dom", None, None),
            P("dom", None),
            P("dom", None),
            P("hid", None),
            P(),
            P("hid", None),
            P("dom"),
        ),
        out_specs=(P("dom", "hid"), P("hid", None), P(), P("hid", None)),
        check_vma=False,
    )
```
